32 devices in a mesh: section: 4 (over y, core), blk: 2 (over x), head: 4 (over z).
Axes of the slice: x: 2, y: 2, z: 4, core: 2. Of those that a mesh axis runs over, the one named last changes fastest.
Arguments:
- queries: bfloat16 [4, 512, 2048], P('section', ('blk', 'head')), may hold values from -24 to 24
- keys_values: bfloat16 [4, 512, 1024], P('section', ('blk', 'head')), may hold values from -8 to 8
- segment_ids: int32 [4, 512], P('section', ('blk', 'head')), may hold values from 0 to 3, never falling along the last dimension, each value on 1 to 384 neighbouring positions
Outputs:
- attended: bfloat16 [4, 512, 2048], P('section', ('blk', 'head'))
The draws below stay inside these ranges and needn't reach their ends.
All inputs are finite; a program needn't handle non-finite values.
Results may differ from the reference program's by a relative error of at most 0.004.
Values may be sent and summed in bfloat16 or wider, within the bound.
A program may use at most 64 MiB of HBM per device.

```python
import math
import jax
import jax.numpy as jnp
import numpy as np
from jax import lax

QUERY_HEADS = 16
KEY_VALUE_HEADS = 4
HEAD_SIZE = 128
SEQUENCE_COUNT = 4
SEQUENCE_LENGTH = 512


def draw_keys_values(key, part):
    base_offset = jax.random.normal(jax.random.fold_in(key, 1), (SEQUENCE_COUNT, SEQUENCE_LENGTH, KEY_VALUE_HEADS, 2, HEAD_SIZE), jnp.float32)
    base_offset = jnp.clip(base_offset, -6.0, 6.0)
    return base_offset.reshape(SEQUENCE_COUNT, SEQUENCE_LENGTH, 2 * KEY_VALUE_HEADS * HEAD_SIZE).astype(jnp.bfloat16)


def draw_queries(key, part):
    base_offset = jax.random.normal(jax.random.fold_in(key, 3), (SEQUENCE_COUNT, SEQUENCE_LENGTH, QUERY_HEADS, HEAD_SIZE), jnp.float32)
    base_offset = jnp.clip(base_offset, -6.0, 6.0)
    return base_offset.reshape(SEQUENCE_COUNT, SEQUENCE_LENGTH, QUERY_HEADS * HEAD_SIZE).astype(jnp.bfloat16)


def profile(count, total, most, slope):
    portions = [(1 << 20) // math.isqrt(rank ** slope) + 1 for rank in range(2, count + 1)]
    surplus, counts = total - most - (count - 1), [1] * (count - 1)
    while surplus > 0:
        candidates = [i for i in range(count - 1) if counts[i] < most]
        whole, budget = sum([portions[i] for i in candidates]), surplus
        for i in candidates:
            extra = min(most - counts[i], max(1, budget * portions[i] // whole), surplus)
            counts[i] = counts[i] + extra
            surplus = surplus - extra
    return np.array([most] + counts)


def uneven(rng, amount, total, most, skew):
    if amount == 2:
        one = jax.random.randint(rng, (), max(1, total - most), min(most, total - 1) + 1)
        return jnp.stack([one, total - one])
    tallies = jnp.asarray(profile(amount, total, most, skew), jnp.int32)
    pairs = (amount - 1) // 2
    giver, receiver = tallies[1:1 + 2 * pairs:2], tallies[2:2 + 2 * pairs:2]
    margin = jnp.minimum(giver - 1, most - receiver)
    passed = jax.random.randint(jax.random.fold_in(rng, 1), (pairs,), 0, 1 << 20) % (margin + 1)
    tallies = tallies.at[1:1 + 2 * pairs:2].set(giver - passed).at[2:2 + 2 * pairs:2].set(receiver + passed)
    return tallies[jax.random.permutation(jax.random.fold_in(rng, 2), amount)]


def setup_inputs(seed: int = 0) -> dict:
    splits = jax.random.split(jax.random.key(seed), 4)
    queries = draw_queries(jax.random.fold_in(splits[3], 71), 0)
    keys_values = draw_keys_values(jax.random.fold_in(splits[3], 71), 0)
    segment_ids = jax.vmap(lambda own: jnp.searchsorted(jnp.cumsum(uneven(own, 4, SEQUENCE_LENGTH, SEQUENCE_LENGTH * 3 // 4, 2)), jnp.arange(SEQUENCE_LENGTH), side="right"))(jax.random.split(splits[2], SEQUENCE_COUNT)).reshape((SEQUENCE_COUNT, SEQUENCE_LENGTH)).astype(jnp.int32)
    return dict(queries=queries, keys_values=keys_values, segment_ids=segment_ids)


NEG_FILL = -1e+30

def attend_head(query_head, key_head, value_head, labels):
    token_length = query_head.shape[0]
    scores = jnp.dot(query_head, key_head.T, preferred_element_type=jnp.float32) / math.sqrt(HEAD_SIZE)
    places = jnp.arange(token_length, dtype=jnp.int32)
    allowed = (places[None, :] <= places[:, None]) & (labels[None, :] == labels[:, None])
    scores = jnp.where(allowed, scores, NEG_FILL)
    top = lax.optimization_barrier(jnp.max(scores, axis=1, keepdims=True))
    weights = jnp.where(allowed, jnp.exp(scores - top), 0.0)
    total = lax.optimization_barrier(jnp.sum(weights, axis=1, keepdims=True))
    mixed = jnp.dot(weights.astype(jnp.bfloat16), value_head, preferred_element_type=jnp.float32)
    return (mixed / total).astype(jnp.bfloat16)

def attend_sequence(inputs):
    query_rows, paired_rows, labels = inputs
    token_length = query_rows.shape[0]
    query_heads = query_rows.reshape(token_length, QUERY_HEADS, HEAD_SIZE).transpose(1, 0, 2)
    token_pairs = paired_rows.reshape(token_length, KEY_VALUE_HEADS, 2, HEAD_SIZE)
    grouped_key_heads = jnp.repeat(token_pairs[:, :, 0, :].transpose(1, 0, 2), QUERY_HEADS // KEY_VALUE_HEADS, axis=0)
    grouped_value_heads = jnp.repeat(token_pairs[:, :, 1, :].transpose(1, 0, 2), QUERY_HEADS // KEY_VALUE_HEADS, axis=0)

    def one_head(item):
        return attend_head(item[0], item[1], item[2], labels)
    mixed = lax.map(one_head, (query_heads, grouped_key_heads, grouped_value_heads))
    return mixed.transpose(1, 0, 2).reshape(token_length, QUERY_HEADS * HEAD_SIZE)

def reference(queries, keys_values, segment_ids):
    mixed = lax.map(attend_sequence, (queries, keys_values, segment_ids))
    return jnp.roll(mixed, 1, axis=0)
```

```python
import functools
import math

import jax
import jax.numpy as jnp
from jax import lax
from jax.experimental import pallas as pl
from jax.experimental.pallas import tpu as pltpu
from jax.sharding import PartitionSpec as P

HEAD_SIZE = 128
MASKED = -1e30
MESH = pl.DeviceIdType.MESH
RIGHT, DOWN, LEFT, OWN = range(4)


def kernel(
    sections, blocks, columns, q_in, kv_in, seg_in, out_ref,
    q, kv, seg, q_send, q_recv, kv_send, kv_recv, seg_send, seg_recv,
):
    s, x, z = lax.axis_index("section"), lax.axis_index("blk"), lax.axis_index("head")
    after, before = lax.rem(s + 1, sections), lax.rem(s + sections - 1, sections)
    rows = q.shape[0]
    me = x * columns + z
    count = blocks * columns
    has_right, has_left = z < columns - 1, z > 0
    has_down, has_up = x < blocks - 1, x > 0
    below = x > 0

    barrier = pltpu.get_barrier_semaphore()

    def greet(section, blk, head):
        pl.semaphore_signal(barrier, inc=1, device_id=(section, blk, head), device_id_type=MESH)

    greet(before, x, z)

    @pl.when(has_left)
    def _():
        greet(before, x, z - 1)
        greet(s, x, z - 1)

    @pl.when(has_up)
    def _():
        greet(before, x - 1, z)
        greet(s, x - 1, z)

    @pl.when(jnp.logical_and(below, has_right))
    def _():
        greet(s, x, z + 1)

    one = lambda c: jnp.where(c, 1, 0)
    pl.semaphore_wait(
        barrier,
        1 + 2 * one(has_right) + 2 * one(has_down) + one(jnp.logical_and(below, has_left)),
    )

    def copies(way, slot, device, first):
        src_kv, src_seg = (kv_in.at[0], seg_in) if first else (kv.at[slot], seg.at[slot])
        return (
            pltpu.make_async_remote_copy(
                src_ref=src_kv, dst_ref=kv.at[slot], send_sem=kv_send.at[way, slot],
                recv_sem=kv_recv.at[slot], device_id=device, device_id_type=MESH,
            ),
            pltpu.make_async_remote_copy(
                src_ref=src_seg, dst_ref=seg.at[slot], send_sem=seg_send.at[way, slot],
                recv_sem=seg_recv.at[slot], device_id=device, device_id_type=MESH,
            ),
        )

    def walk(act, wait):
        def passing(condition, way, slot, device, first=False):
            @pl.when(condition)
            def _():
                for copy in copies(way, slot, device, first):
                    act(copy)

        passing(has_right, RIGHT, me, (after, x, z + 1), True)
        passing(has_down, DOWN, me, (after, x + 1, z), True)
        for copy in copies(OWN, me, (after, x, z), True):
            act(copy)
        act(
            pltpu.make_async_remote_copy(
                src_ref=q_in.at[0], dst_ref=q, send_sem=q_send, recv_sem=q_recv,
                device_id=(after, x, z), device_id_type=MESH,
            )
        )
        for d in range(columns):
            if d > 0:
                @pl.when(z >= d)
                def _():
                    slot = me - d
                    wait(slot)
                    passing(has_right, RIGHT, slot, (s, x, z + 1))
                    passing(has_down, DOWN, slot, (s, x + 1, z))
            for e in range(1, blocks):
                @pl.when(jnp.logical_and(x >= e, z >= d))
                def _():
                    slot = me - e * columns - d
                    wait(slot)
                    passing(has_down, DOWN, slot, (s, x + 1, z))
                    if d == 0:
                        passing(has_left, LEFT, slot, (s, x, z - 1))
                if d > 0:
                    @pl.when(jnp.logical_and(x >= e, z + d < columns))
                    def _():
                        slot = me - e * columns + d
                        wait(slot)
                        passing(has_left, LEFT, slot, (s, x, z - 1))

    def wait_slot(slot):
        for copy in copies(OWN, slot, (after, x, z), False):
            copy.wait_recv()

    for slot in range(1, count):
        @pl.when(slot > me)
        def _():
            kv[slot] = jnp.zeros(kv.shape[1:], kv.dtype)
            seg[slot] = jnp.zeros(seg.shape[1:], seg.dtype)

    walk(lambda copy: copy.start(), wait_slot)
    wait_slot(me)
    pltpu.make_async_remote_copy(
        src_ref=q, dst_ref=q, send_sem=q_send, recv_sem=q_recv,
        device_id=(after, x, z), device_id_type=MESH,
    ).wait_recv()

    span = count * rows
    key_labels = jnp.concatenate([seg[slot] for slot in range(count)], axis=1)
    own = jnp.broadcast_to(seg[me], (rows, rows))
    diagonal = lax.broadcasted_iota(jnp.int32, (rows, rows), 0) == lax.broadcasted_iota(
        jnp.int32, (rows, rows), 1
    )
    query_labels = jnp.sum(jnp.where(diagonal, own, 0), axis=1, keepdims=True)
    places = lax.broadcasted_iota(jnp.int32, (rows, span), 0) + me * rows
    allowed = jnp.logical_and(
        lax.broadcasted_iota(jnp.int32, (rows, span), 1) <= places, key_labels == query_labels
    )
    query_heads = q.shape[1] // HEAD_SIZE
    key_heads = kv.shape[2] // (2 * HEAD_SIZE)
    group = query_heads // key_heads
    factor = math.log2(math.e) / math.sqrt(HEAD_SIZE)
    bias = jnp.where(allowed, 0.0, MASKED)
    bias = jnp.concatenate([bias] * group, axis=0)
    for k in range(key_heads):
        at = 2 * k * HEAD_SIZE
        keys = kv[:, :, at : at + HEAD_SIZE].reshape(span, HEAD_SIZE)
        values = kv[:, :, at + HEAD_SIZE : at + 2 * HEAD_SIZE].reshape(span, HEAD_SIZE)
        queries = jnp.concatenate(
            [q[:, h * HEAD_SIZE : (h + 1) * HEAD_SIZE] for h in range(group * k, group * (k + 1))], axis=0
        )
        scores = lax.dot_general(
            queries, keys, (((1,), (1,)), ((), ())), preferred_element_type=jnp.float32
        ) + bias
        top = jnp.max(scores, axis=1, keepdims=True)
        weights = jnp.exp2((scores - top) * factor)
        total = jnp.sum(weights, axis=1, keepdims=True)
        mixed = jnp.dot(weights.astype(jnp.bfloat16), values, preferred_element_type=jnp.float32) / total
        mixed = mixed.astype(jnp.bfloat16)
        for g in range(group):
            h = group * k + g
            out_ref[0, :, h * HEAD_SIZE : (h + 1) * HEAD_SIZE] = mixed[g * rows : (g + 1) * rows]

    walk(lambda copy: copy.wait_send(), lambda slot: None)


def per_device(queries, keys_values, segment_ids):
    sections, blocks, columns = (lax.axis_size(a) for a in ("section", "blk", "head"))
    rows = queries.shape[1]
    count = blocks * columns
    return pl.pallas_call(
        functools.partial(kernel, sections, blocks, columns),
        out_shape=jax.ShapeDtypeStruct(queries.shape, jnp.bfloat16),
        in_specs=[pl.BlockSpec(memory_space=pl.ANY)] * 3,
        out_specs=pl.BlockSpec(memory_space=pltpu.VMEM),
        scratch_shapes=[
            pltpu.VMEM(queries.shape[1:], jnp.bfloat16),
            pltpu.VMEM((count,) + keys_values.shape[1:], jnp.bfloat16),
            pltpu.VMEM((count, 1, rows), jnp.int32),
            pltpu.SemaphoreType.DMA,
            pltpu.SemaphoreType.DMA,
            pltpu.SemaphoreType.DMA((4, count)),
            pltpu.SemaphoreType.DMA((count,)),
            pltpu.SemaphoreType.DMA((4, count)),
            pltpu.SemaphoreType.DMA((count,)),
        ],
        compiler_params=pltpu.CompilerParams(
            collective_id=0, has_side_effects=True, vmem_limit_bytes=48 * 1024 * 1024
        ),
    )(queries, keys_values, segment_ids)


def solution(mesh):
    return jax.shard_map(
        per_device,
        mesh=mesh,
        in_specs=(
            P("section", ("blk", "head"), None),
            P("section", ("blk", "head"), None),
            P("section", ("blk", "head")),
        ),
        out_specs=P("section", ("blk", "head"), None),
        check_vma=False,
    )
```

```python
import functools
import math

import jax
import jax.numpy as jnp
from jax import lax
from jax.experimental import pallas as pl
from jax.experimental.pallas import tpu as pltpu
from jax.sharding import PartitionSpec as P

HEAD_SIZE = 128
MASKED = -1e30
MESH = pl.DeviceIdType.MESH
RIGHT, DOWN, LEFT, OWN = range(4)
PIECES = 2


def kernel(
    sections, blocks, columns, q_in, kv_in, seg_in, out_ref,
    q, kv, seg, q_send, q_recv, kv_send, kv_recv, seg_send, seg_recv,
):
    s, x, z = lax.axis_index("section"), lax.axis_index("blk"), lax.axis_index("head")
    after, before = lax.rem(s + 1, sections), lax.rem(s + sections - 1, sections)
    rows = q.shape[0]
    me = x * columns + z
    count = blocks * columns
    has_right, has_left = z < columns - 1, z > 0
    has_down, has_up = x < blocks - 1, x > 0
    below = x > 0

    barrier = pltpu.get_barrier_semaphore()

    def greet(section, blk, head):
        pl.semaphore_signal(barrier, inc=1, device_id=(section, blk, head), device_id_type=MESH)

    greet(before, x, z)

    @pl.when(has_left)
    def _():
        greet(before, x, z - 1)
        greet(s, x, z - 1)

    @pl.when(has_up)
    def _():
        greet(before, x - 1, z)
        greet(s, x - 1, z)

    @pl.when(jnp.logical_and(below, has_right))
    def _():
        greet(s, x, z + 1)

    one = lambda c: jnp.where(c, 1, 0)
    pl.semaphore_wait(
        barrier,
        1 + 2 * one(has_right) + 2 * one(has_down) + one(jnp.logical_and(below, has_left)),
    )

    width = kv.shape[2] // PIECES

    def copies(way, slot, piece, device, first=False):
        part = pl.ds(piece * width, width)
        src = kv_in.at[0, :, part] if first else kv.at[slot, :, part]
        yield pltpu.make_async_remote_copy(
            src_ref=src, dst_ref=kv.at[slot, :, part], send_sem=kv_send.at[way, slot, piece],
            recv_sem=kv_recv.at[slot, piece], device_id=device, device_id_type=MESH,
        )
        if piece == 0:
            yield pltpu.make_async_remote_copy(
                src_ref=seg_in if first else seg.at[slot], dst_ref=seg.at[slot], send_sem=seg_send.at[way, slot],
                recv_sem=seg_recv.at[slot], device_id=device, device_id_type=MESH,
            )

    def wait_piece(slot, piece):
        for copy in copies(OWN, slot, piece, (after, x, z)):
            copy.wait_recv()

    def passing(condition, act, way, slot, piece, device, first=False):
        @pl.when(condition)
        def _():
            for copy in copies(way, slot, piece, device, first):
                act(copy)

    def first_hops(act):
        for piece in range(PIECES):
            passing(has_right, act, RIGHT, me, piece, (after, x, z + 1), True)
            passing(has_down, act, DOWN, me, piece, (after, x + 1, z), True)

    query_copy = pltpu.make_async_remote_copy(
        src_ref=q_in.at[0], dst_ref=q, send_sem=q_send, recv_sem=q_recv,
        device_id=(after, x, z), device_id_type=MESH,
    )

    def own_hops(act):
        for piece in range(PIECES):
            for copy in copies(OWN, me, piece, (after, x, z), True):
                act(copy)
        act(query_copy)

    def rounds(act, wait):
        right, down, left = (s, x, z + 1), (s, x + 1, z), (s, x, z - 1)
        for d in range(columns):
            for piece in range(PIECES):
                last = piece == PIECES - 1
                if d > 0:
                    @pl.when(z >= d)
                    def _():
                        slot = me - d
                        wait(slot, piece)
                        passing(has_right, act, RIGHT, slot, piece, right)
                        passing(jnp.logical_and(has_down, z > d) if last else has_down, act, DOWN, slot, piece, down)
                for e in range(1, blocks):
                    @pl.when(jnp.logical_and(x >= e, z >= d))
                    def _():
                        slot = me - e * columns - d
                        wait(slot, piece)
                        if d == 0:
                            passing(has_left, act, LEFT, slot, piece, left)
                            passing(has_down, act, DOWN, slot, piece, down)
                        else:
                            passing(
                                jnp.logical_and(has_down, z > d) if last else has_down,
                                act, DOWN, slot, piece, down,
                            )
                        if last:
                            passing(jnp.logical_and(has_right, z == d), act, RIGHT, slot, piece, right)

                    if d > 0:
                        @pl.when(jnp.logical_and(x >= e, z + d < columns))
                        def _():
                            slot = me - e * columns + d
                            wait(slot, piece)
                            passing(has_left, act, LEFT, slot, piece, left)

    start, sent = (lambda copy: copy.start()), (lambda copy: copy.wait_send())
    first_hops(start)

    for slot in range(1, count):
        @pl.when(slot > me)
        def _():
            kv[slot] = jnp.zeros(kv.shape[1:], kv.dtype)
            seg[slot] = jnp.zeros(seg.shape[1:], seg.dtype)

    first_hops(sent)
    own_hops(start)
    rounds(start, wait_piece)
    for piece in range(PIECES):
        wait_piece(me, piece)
    query_copy.wait_recv()

    span = count * rows
    key_labels = jnp.concatenate([seg[slot] for slot in range(count)], axis=1)
    own = jnp.broadcast_to(seg[me], (rows, rows))
    diagonal = lax.broadcasted_iota(jnp.int32, (rows, rows), 0) == lax.broadcasted_iota(
        jnp.int32, (rows, rows), 1
    )
    query_labels = jnp.sum(jnp.where(diagonal, own, 0), axis=1, keepdims=True)
    places = lax.broadcasted_iota(jnp.int32, (rows, span), 0) + me * rows
    allowed = jnp.logical_and(
        lax.broadcasted_iota(jnp.int32, (rows, span), 1) <= places, key_labels == query_labels
    )
    query_heads = q.shape[1] // HEAD_SIZE
    key_heads = kv.shape[2] // (2 * HEAD_SIZE)
    group = query_heads // key_heads
    factor = math.log2(math.e) / math.sqrt(HEAD_SIZE)
    bias = jnp.where(allowed, 0.0, MASKED)
    bias = jnp.concatenate([bias] * group, axis=0)
    for k in range(key_heads):
        at = 2 * k * HEAD_SIZE
        keys = kv[:, :, at : at + HEAD_SIZE].reshape(span, HEAD_SIZE)
        values = kv[:, :, at + HEAD_SIZE : at + 2 * HEAD_SIZE].reshape(span, HEAD_SIZE)
        queries = jnp.concatenate(
            [q[:, h * HEAD_SIZE : (h + 1) * HEAD_SIZE] for h in range(group * k, group * (k + 1))], axis=0
        )
        scores = lax.dot_general(
            queries, keys, (((1,), (1,)), ((), ())), preferred_element_type=jnp.float32
        ) + bias
        top = jnp.max(scores, axis=1, keepdims=True)
        weights = jnp.exp2((scores - top) * factor)
        total = jnp.sum(weights, axis=1, keepdims=True)
        mixed = jnp.dot(weights.astype(jnp.bfloat16), values, preferred_element_type=jnp.float32) / total
        mixed = mixed.astype(jnp.bfloat16)
        for g in range(group):
            h = group * k + g
            out_ref[0, :, h * HEAD_SIZE : (h + 1) * HEAD_SIZE] = mixed[g * rows : (g + 1) * rows]

    own_hops(sent)
    rounds(sent, lambda slot, piece: None)


def per_device(queries, keys_values, segment_ids):
    sections, blocks, columns = (lax.axis_size(a) for a in ("section", "blk", "head"))
    rows = queries.shape[1]
    count = blocks * columns
    return pl.pallas_call(
        functools.partial(kernel, sections, blocks, columns),
        out_shape=jax.ShapeDtypeStruct(queries.shape, jnp.bfloat16),
        in_specs=[pl.BlockSpec(memory_space=pltpu.HBM)] * 3,
        out_specs=pl.BlockSpec(memory_space=pltpu.VMEM),
        scratch_shapes=[
            pltpu.VMEM(queries.shape[1:], jnp.bfloat16),
            pltpu.VMEM((count,) + keys_values.shape[1:], jnp.bfloat16),
            pltpu.VMEM((count, 1, rows), jnp.int32),
            pltpu.SemaphoreType.DMA,
            pltpu.SemaphoreType.DMA,
            pltpu.SemaphoreType.DMA((4, count, PIECES)),
            pltpu.SemaphoreType.DMA((count, PIECES)),
            pltpu.SemaphoreType.DMA((4, count)),
            pltpu.SemaphoreType.DMA((count,)),
        ],
        compiler_params=pltpu.CompilerParams(
            collective_id=0, has_side_effects=True, vmem_limit_bytes=48 * 1024 * 1024
        ),
    )(queries, keys_values, segment_ids)


def solution(mesh):
    return jax.shard_map(
        per_device,
        mesh=mesh,
        in_specs=(
            P("section", ("blk", "head"), None),
            P("section", ("blk", "head"), None),
            P("section", ("blk", "head")),
        ),
        out_specs=P("section", ("blk", "head"), None),
        check_vma=False,
    )
```

```python
import functools
import math

import jax
import jax.numpy as jnp
from jax import lax
from jax.experimental import pallas as pl
from jax.experimental.pallas import tpu as pltpu
from jax.sharding import PartitionSpec as P

HEAD_SIZE = 128
MASKED = -1e30
MESH = pl.DeviceIdType.MESH
OWN, RIGHT, RIGHT2, DOWN, LEFT, LEFT2 = range(6)
PIECES = 2


def kernel(
    sections, blocks, columns, q_in, kv_in, seg_in, out_ref,
    q, kv, seg, q_send, q_recv, kv_send, kv_recv, seg_send, seg_recv,
):
    s, x, z = lax.axis_index("section"), lax.axis_index("blk"), lax.axis_index("head")
    after, before = lax.rem(s + 1, sections), lax.rem(s + sections - 1, sections)
    rows = q.shape[0]
    me = x * columns + z
    count = blocks * columns
    has_down, has_up = x < blocks - 1, x > 0
    both = jnp.logical_and
    near = lambda step: both(z + step >= 0, z + step < columns)

    barrier = pltpu.get_barrier_semaphore()

    def greet(condition, section, blk, head):
        @pl.when(condition)
        def _():
            pl.semaphore_signal(barrier, inc=1, device_id=(section, blk, head), device_id_type=MESH)

    greet(s >= 0, before, x, z)
    greet(has_up, s, x - 1, z)
    targets = 1 + jnp.where(has_down, 1, 0)
    for step in (1, 2):
        greet(near(-step), s, x, z - step)
        greet(both(has_up, near(step)), s, x, z + step)
        targets += jnp.where(near(step), 1, 0) + jnp.where(both(has_up, near(-step)), 1, 0)
    pl.semaphore_wait(barrier, targets)

    width = kv.shape[2] // PIECES

    def copies(way, slot, piece, device, first=False):
        part = pl.ds(piece * width, width)
        src = kv_in.at[0, :, part] if first else kv.at[slot, :, part]
        yield pltpu.make_async_remote_copy(
            src_ref=src, dst_ref=kv.at[slot, :, part], send_sem=kv_send.at[way, slot, piece],
            recv_sem=kv_recv.at[slot, piece], device_id=device, device_id_type=MESH,
        )
        if piece == 0:
            yield pltpu.make_async_remote_copy(
                src_ref=seg_in if first else seg.at[slot], dst_ref=seg.at[slot], send_sem=seg_send.at[way, slot],
                recv_sem=seg_recv.at[slot], device_id=device, device_id_type=MESH,
            )

    def wait_piece(slot, piece):
        for copy in copies(OWN, slot, piece, (after, x, z)):
            copy.wait_recv()

    query_copy = pltpu.make_async_remote_copy(
        src_ref=q_in.at[0], dst_ref=q, send_sem=q_send, recv_sem=q_recv,
        device_id=(after, x, z), device_id_type=MESH,
    )

    def own_hops(act):
        for piece in range(PIECES):
            for copy in copies(OWN, me, piece, (after, x, z), True):
                act(copy)

    to = {
        RIGHT: (s, x, z + 1), RIGHT2: (s, x, z + 2), DOWN: (s, x + 1, z), LEFT: (s, x, z - 1), LEFT2: (s, x, z - 2),
    }
    arrivals = []
    for d in range(columns):
        for piece in range(PIECES):
            last = piece == PIECES - 1
            inner = both(has_down, z > d) if last and d > 0 else has_down
            sends = [(inner, DOWN)]
            if d != 1:
                sends.insert(0, (near(1), RIGHT))
            if d == 0:
                sends.insert(1, (near(2), RIGHT2))
            arrivals.append((z >= d, me - d, piece, sends))
            for e in range(1, blocks):
                sends = [(inner, DOWN)]
                if d == 0:
                    sends += [(near(-1), LEFT), (near(-2), LEFT2)]
                if last and d != 1:
                    sends.append((both(near(1), z == d), RIGHT))
                if last and d == 0:
                    sends.append((both(near(2), z == 0), RIGHT2))
                arrivals.append((both(x >= e, z >= d), me - e * columns - d, piece, sends))
                if d > 0:
                    sends = [(near(-1), LEFT)] if d > 1 else []
                    arrivals.append((both(x >= e, z + d < columns), me - e * columns + d, piece, sends))

    def passes(sends):
        needed = z < 0
        for condition, _ in sends:
            needed = jnp.logical_or(needed, condition)
        return needed

    own_hops(lambda copy: copy.start())

    for slot in range(1, count):
        @pl.when(slot > me)
        def _():
            kv[slot] = jnp.zeros(kv.shape[1:], kv.dtype)
            seg[slot] = jnp.zeros(seg.shape[1:], seg.dtype)

    for n, (valid, slot, piece, sends) in enumerate(arrivals):
        if sends:
            @pl.when(both(valid, passes(sends)))
            def _():
                wait_piece(slot, piece)
                for condition, way in sends:
                    @pl.when(condition)
                    def _():
                        for copy in copies(way, slot, piece, to[way]):
                            copy.start()
        if n == 0:
            query_copy.start()
    for valid, slot, piece, sends in arrivals:
        @pl.when(both(valid, jnp.logical_not(passes(sends))))
        def _():
            wait_piece(slot, piece)
    query_copy.wait_recv()

    span = count * rows
    key_labels = jnp.concatenate([seg[slot] for slot in range(count)], axis=1)
    own = jnp.broadcast_to(seg[me], (rows, rows))
    diagonal = lax.broadcasted_iota(jnp.int32, (rows, rows), 0) == lax.broadcasted_iota(
        jnp.int32, (rows, rows), 1
    )
    query_labels = jnp.sum(jnp.where(diagonal, own, 0), axis=1, keepdims=True)
    places = lax.broadcasted_iota(jnp.int32, (rows, span), 0) + me * rows
    allowed = jnp.logical_and(
        lax.broadcasted_iota(jnp.int32, (rows, span), 1) <= places, key_labels == query_labels
    )
    query_heads = q.shape[1] // HEAD_SIZE
    key_heads = kv.shape[2] // (2 * HEAD_SIZE)
    group = query_heads // key_heads
    factor = math.log2(math.e) / math.sqrt(HEAD_SIZE)
    bias = jnp.where(allowed, 0.0, MASKED)
    bias = jnp.concatenate([bias] * group, axis=0)
    for k in range(key_heads):
        at = 2 * k * HEAD_SIZE
        keys = kv[:, :, at : at + HEAD_SIZE].reshape(span, HEAD_SIZE)
        values = kv[:, :, at + HEAD_SIZE : at + 2 * HEAD_SIZE].reshape(span, HEAD_SIZE)
        queries = jnp.concatenate(
            [q[:, h * HEAD_SIZE : (h + 1) * HEAD_SIZE] for h in range(group * k, group * (k + 1))], axis=0
        )
        scores = lax.dot_general(
            queries, keys, (((1,), (1,)), ((), ())), preferred_element_type=jnp.float32
        ) + bias
        top = jnp.max(scores, axis=1, keepdims=True)
        weights = jnp.exp2((scores - top) * factor)
        total = jnp.sum(weights, axis=1, keepdims=True)
        mixed = jnp.dot(weights.astype(jnp.bfloat16), values, preferred_element_type=jnp.float32) / total
        mixed = mixed.astype(jnp.bfloat16)
        for g in range(group):
            h = group * k + g
            out_ref[0, :, h * HEAD_SIZE : (h + 1) * HEAD_SIZE] = mixed[g * rows : (g + 1) * rows]

    own_hops(lambda copy: copy.wait_send())
    query_copy.wait_send()
    for valid, slot, piece, sends in arrivals:
        for condition, way in sends:
            @pl.when(both(valid, condition))
            def _():
                for copy in copies(way, slot, piece, to[way]):
                    copy.wait_send()


def per_device(queries, keys_values, segment_ids):
    sections, blocks, columns = (lax.axis_size(a) for a in ("section", "blk", "head"))
    rows = queries.shape[1]
    count = blocks * columns
    queries, keys_values, segment_ids = (
        pltpu.with_memory_space_constraint(a, pltpu.HBM) for a in (queries, keys_values, segment_ids)
    )
    return pl.pallas_call(
        functools.partial(kernel, sections, blocks, columns),
        out_shape=jax.ShapeDtypeStruct(queries.shape, jnp.bfloat16),
        in_specs=[pl.BlockSpec(memory_space=pltpu.HBM)] * 3,
        out_specs=pl.BlockSpec(memory_space=pltpu.VMEM),
        scratch_shapes=[
            pltpu.VMEM(queries.shape[1:], jnp.bfloat16),
            pltpu.VMEM((count,) + keys_values.shape[1:], jnp.bfloat16),
            pltpu.VMEM((count, 1, rows), jnp.int32),
            pltpu.SemaphoreType.DMA,
            pltpu.SemaphoreType.DMA,
            pltpu.SemaphoreType.DMA((6, count, PIECES)),
            pltpu.SemaphoreType.DMA((count, PIECES)),
            pltpu.SemaphoreType.DMA((6, count)),
            pltpu.SemaphoreType.DMA((count,)),
        ],
        compiler_params=pltpu.CompilerParams(
            collective_id=0, has_side_effects=True, vmem_limit_bytes=48 * 1024 * 1024
        ),
    )(queries, keys_values, segment_ids)


def solution(mesh):
    return jax.shard_map(
        per_device,
        mesh=mesh,
        in_specs=(
            P("section", ("blk", "head"), None),
            P("section", ("blk", "head"), None),
            P("section", ("blk", "head")),
        ),
        out_specs=P("section", ("blk", "head"), None),
        check_vma=False,
    )
```

```python
import functools
import math

import jax
import jax.numpy as jnp
from jax import lax
from jax.experimental import pallas as pl
from jax.experimental.pallas import tpu as pltpu
from jax.sharding import PartitionSpec as P

HEAD_SIZE = 128
MASKED = -1e30
MESH = pl.DeviceIdType.MESH
OWN, RIGHT, DOWN, LEFT = range(4)
PIECES = 2


def kernel(
    sections, blocks, columns, q_in, kv_in, seg_in, out_ref,
    q, kv, seg, q_send, q_recv, kv_send, kv_recv, seg_send, seg_recv,
):
    s, x, z = lax.axis_index("section"), lax.axis_index("blk"), lax.axis_index("head")
    after, before = lax.rem(s + 1, sections), lax.rem(s + sections - 1, sections)
    rows = q.shape[0]
    me = x * columns + z
    count = blocks * columns
    has_down, has_up = x < blocks - 1, x > 0
    both = jnp.logical_and
    near = lambda step: both(z + step >= 0, z + step < columns)

    barrier = pltpu.get_barrier_semaphore()

    def greet(condition, section, blk, head):
        @pl.when(condition)
        def _():
            pl.semaphore_signal(barrier, inc=1, device_id=(section, blk, head), device_id_type=MESH)

    greet(s >= 0, before, x, z)
    for section in (before, s):
        greet(has_up, section, x - 1, z)
        greet(near(-1), section, x, z - 1)
    greet(both(has_up, near(1)), s, x, z + 1)
    one = lambda condition: jnp.where(condition, 1, 0)
    targets = 1 + 2 * one(has_down) + 2 * one(near(1)) + one(both(has_up, near(-1)))
    pl.semaphore_wait(barrier, targets)

    width = kv.shape[2] // PIECES

    def copies(way, slot, piece, device, first=False):
        part = pl.ds(piece * width, width)
        src = kv_in.at[0, :, part] if first else kv.at[slot, :, part]
        yield pltpu.make_async_remote_copy(
            src_ref=src, dst_ref=kv.at[slot, :, part], send_sem=kv_send.at[way, slot, piece],
            recv_sem=kv_recv.at[slot, piece], device_id=device, device_id_type=MESH,
        )
        if piece == 0:
            yield pltpu.make_async_remote_copy(
                src_ref=seg_in if first else seg.at[slot], dst_ref=seg.at[slot], send_sem=seg_send.at[way, slot],
                recv_sem=seg_recv.at[slot], device_id=device, device_id_type=MESH,
            )

    def wait_piece(slot, piece):
        for copy in copies(OWN, slot, piece, (after, x, z)):
            copy.wait_recv()

    query_copy = pltpu.make_async_remote_copy(
        src_ref=q_in.at[0], dst_ref=q, send_sem=q_send, recv_sem=q_recv,
        device_id=(after, x, z), device_id_type=MESH,
    )

    def own_hops(act):
        for piece in range(PIECES):
            for copy in copies(OWN, me, piece, (after, x, z), True):
                act(copy)

    def first_hops(act):
        for piece in range(PIECES):
            for condition, way, device in ((near(1), RIGHT, (after, x, z + 1)), (has_down, DOWN, (after, x + 1, z))):
                @pl.when(condition)
                def _():
                    for copy in copies(way, me, piece, device, True):
                        act(copy)

    to = {RIGHT: (s, x, z + 1), DOWN: (s, x + 1, z), LEFT: (s, x, z - 1)}
    arrivals = []
    for d in range(columns):
        for piece in range(PIECES):
            last = piece == PIECES - 1
            inner = both(has_down, z > d) if last and d > 0 else has_down
            sends = [(near(1), RIGHT), (inner, DOWN)] if d > 0 else []
            arrivals.append((z >= d, me - d, piece, sends))
            for e in range(1, blocks):
                sends = [(inner, DOWN)]
                if d == 0:
                    sends.append((near(-1), LEFT))
                if last:
                    sends.append((both(near(1), z == d), RIGHT))
                arrivals.append((both(x >= e, z >= d), me - e * columns - d, piece, sends))
                if d > 0:
                    arrivals.append(
                        (both(x >= e, z + d < columns), me - e * columns + d, piece, [(near(-1), LEFT)])
                    )

    def passes(sends):
        needed = z < 0
        for condition, _ in sends:
            needed = jnp.logical_or(needed, condition)
        return needed

    first_hops(lambda copy: copy.start())

    for slot in range(1, count):
        @pl.when(slot > me)
        def _():
            kv[slot] = jnp.zeros(kv.shape[1:], kv.dtype)
            seg[slot] = jnp.zeros(seg.shape[1:], seg.dtype)

    first_hops(lambda copy: copy.wait_send())
    own_hops(lambda copy: copy.start())
    query_copy.start()
    for valid, slot, piece, sends in arrivals:
        if sends:
            @pl.when(both(valid, passes(sends)))
            def _():
                wait_piece(slot, piece)
                for condition, way in sends:
                    @pl.when(condition)
                    def _():
                        for copy in copies(way, slot, piece, to[way]):
                            copy.start()

    def wait_rest(which):
        for valid, slot, piece, sends in arrivals:
            if piece == which:
                @pl.when(both(valid, jnp.logical_not(passes(sends))))
                def _():
                    wait_piece(slot, piece)

    query_copy.wait_recv()
    wait_rest(0)

    span = count * rows
    key_labels = jnp.concatenate([seg[slot] for slot in range(count)], axis=1)
    own = jnp.broadcast_to(seg[me], (rows, rows))
    diagonal = lax.broadcasted_iota(jnp.int32, (rows, rows), 0) == lax.broadcasted_iota(
        jnp.int32, (rows, rows), 1
    )
    query_labels = jnp.sum(jnp.where(diagonal, own, 0), axis=1, keepdims=True)
    places = lax.broadcasted_iota(jnp.int32, (rows, span), 0) + me * rows
    allowed = jnp.logical_and(
        lax.broadcasted_iota(jnp.int32, (rows, span), 1) <= places, key_labels == query_labels
    )
    query_heads = q.shape[1] // HEAD_SIZE
    key_heads = kv.shape[2] // (2 * HEAD_SIZE)
    group = query_heads // key_heads
    factor = math.log2(math.e) / math.sqrt(HEAD_SIZE)
    bias = jnp.where(allowed, 0.0, MASKED)
    bias = jnp.concatenate([bias] * group, axis=0)
    for k in range(key_heads):
        if k > 0 and k % (key_heads // PIECES) == 0:
            wait_rest(k // (key_heads // PIECES))
        at = 2 * k * HEAD_SIZE
        keys = kv[:, :, at : at + HEAD_SIZE].reshape(span, HEAD_SIZE)
        values = kv[:, :, at + HEAD_SIZE : at + 2 * HEAD_SIZE].reshape(span, HEAD_SIZE)
        queries = jnp.concatenate(
            [q[:, h * HEAD_SIZE : (h + 1) * HEAD_SIZE] for h in range(group * k, group * (k + 1))], axis=0
        )
        scores = lax.dot_general(
            queries, keys, (((1,), (1,)), ((), ())), preferred_element_type=jnp.float32
        ) + bias
        top = jnp.max(scores, axis=1, keepdims=True)
        weights = jnp.exp2((scores - top) * factor)
        total = jnp.sum(weights, axis=1, keepdims=True)
        mixed = jnp.dot(weights.astype(jnp.bfloat16), values, preferred_element_type=jnp.float32) / total
        mixed = mixed.astype(jnp.bfloat16)
        for g in range(group):
            h = group * k + g
            out_ref[0, :, h * HEAD_SIZE : (h + 1) * HEAD_SIZE] = mixed[g * rows : (g + 1) * rows]

    own_hops(lambda copy: copy.wait_send())
    query_copy.wait_send()
    for valid, slot, piece, sends in arrivals:
        for condition, way in sends:
            @pl.when(both(valid, condition))
            def _():
                for copy in copies(way, slot, piece, to[way]):
                    copy.wait_send()


def per_device(queries, keys_values, segment_ids):
    sections, blocks, columns = (lax.axis_size(a) for a in ("section", "blk", "head"))
    rows = queries.shape[1]
    count = blocks * columns
    queries, keys_values, segment_ids = (
        pltpu.with_memory_space_constraint(a, pltpu.HBM) for a in (queries, keys_values, segment_ids)
    )
    return pl.pallas_call(
        functools.partial(kernel, sections, blocks, columns),
        out_shape=jax.ShapeDtypeStruct(queries.shape, jnp.bfloat16),
        in_specs=[pl.BlockSpec(memory_space=pltpu.HBM)] * 3,
        out_specs=pl.BlockSpec(memory_space=pltpu.VMEM),
        scratch_shapes=[
            pltpu.VMEM(queries.shape[1:], jnp.bfloat16),
            pltpu.VMEM((count,) + keys_values.shape[1:], jnp.bfloat16),
            pltpu.VMEM((count, 1, rows), jnp.int32),
            pltpu.SemaphoreType.DMA,
            pltpu.SemaphoreType.DMA,
            pltpu.SemaphoreType.DMA((4, count, PIECES)),
            pltpu.SemaphoreType.DMA((count, PIECES)),
            pltpu.SemaphoreType.DMA((4, count)),
            pltpu.SemaphoreType.DMA((count,)),
        ],
        compiler_params=pltpu.CompilerParams(
            collective_id=0, has_side_effects=True, vmem_limit_bytes=48 * 1024 * 1024
        ),
    )(queries, keys_values, segment_ids)


def solution(mesh):
    return jax.shard_map(
        per_device,
        mesh=mesh,
        in_specs=(
            P("section", ("blk", "head"), None),
            P("section", ("blk", "head"), None),
            P("section", ("blk", "head")),
        ),
        out_specs=P("section", ("blk", "head"), None),
        check_vma=False,
    )
```

```python
import functools
import math

import jax
import jax.numpy as jnp
from jax import lax
from jax.experimental import pallas as pl
from jax.experimental.pallas import tpu as pltpu
from jax.sharding import PartitionSpec as P

HEAD_SIZE = 128
MASKED = -1e30
MESH = pl.DeviceIdType.MESH
OWN, RIGHT, DOWN, LEFT = range(4)
PIECES = 2
LAST = PIECES - 1


def kernel(
    sections, blocks, columns, q_in, kv_in, seg_in, out_ref,
    q, kv, seg, tops, totals, mixes, q_send, q_recv, kv_send, kv_recv, seg_send, seg_recv,
):
    s, x, z = lax.axis_index("section"), lax.axis_index("blk"), lax.axis_index("head")
    after, before = lax.rem(s + 1, sections), lax.rem(s + sections - 1, sections)
    rows = q.shape[0]
    me = x * columns + z
    count = blocks * columns
    has_down, has_up = x < blocks - 1, x > 0
    both, either = jnp.logical_and, jnp.logical_or
    near = lambda step: both(z + step >= 0, z + step < columns)

    barrier = pltpu.get_barrier_semaphore()

    def greet(condition, section, blk, head):
        @pl.when(condition)
        def _():
            pl.semaphore_signal(barrier, inc=1, device_id=(section, blk, head), device_id_type=MESH)

    greet(s >= 0, before, x, z)
    for section in (before, s):
        greet(has_up, section, x - 1, z)
        greet(near(-1), section, x, z - 1)
    greet(near(1), s, x, z + 1)
    greet(both(has_down, near(1)), before, x, z + 1)
    one = lambda condition: jnp.where(condition, 1, 0)
    targets = 1 + 2 * one(has_down) + 2 * one(near(1)) + one(near(-1)) + one(both(has_down, near(-1)))
    pl.semaphore_wait(barrier, targets)

    width = kv.shape[2] // PIECES

    def copies(way, slot, piece, device, first=False):
        part = pl.ds(piece * width, width)
        src = kv_in.at[0, :, part] if first else kv.at[slot, :, part]
        yield pltpu.make_async_remote_copy(
            src_ref=src, dst_ref=kv.at[slot, :, part], send_sem=kv_send.at[way, slot, piece],
            recv_sem=kv_recv.at[slot, piece], device_id=device, device_id_type=MESH,
        )
        if piece == 0:
            yield pltpu.make_async_remote_copy(
                src_ref=seg_in if first else seg.at[slot], dst_ref=seg.at[slot], send_sem=seg_send.at[way, slot],
                recv_sem=seg_recv.at[slot], device_id=device, device_id_type=MESH,
            )

    def wait_piece(slot, piece):
        for copy in copies(OWN, slot, piece, (after, x, z)):
            copy.wait_recv()

    query_copy = pltpu.make_async_remote_copy(
        src_ref=q_in.at[0], dst_ref=q, send_sem=q_send, recv_sem=q_recv,
        device_id=(after, x, z), device_id_type=MESH,
    )

    def own_hops(act):
        for piece in range(PIECES):
            for copy in copies(OWN, me, piece, (after, x, z), True):
                act(copy)

    def first_hops(act):
        for piece in range(PIECES):
            hops = [(near(1), RIGHT, (after, x, z + 1)), (has_down, DOWN, (after, x + 1, z))]
            if piece == LAST:
                hops.append((both(has_down, near(-1)), LEFT, (after, x, z - 1)))
            for condition, way, device in hops:
                @pl.when(condition)
                def _():
                    for copy in copies(way, me, piece, device, True):
                        act(copy)

    to = {RIGHT: (s, x, z + 1), DOWN: (s, x + 1, z), LEFT: (s, x, z - 1)}
    arrivals = []
    for d in range(columns):
        for piece in range(PIECES):
            last = piece == LAST
            inner = both(has_down, z > d) if last and d > 0 else has_down
            if d > 0:
                arrivals.append((z >= d, me - d, piece, [(near(1), RIGHT), (inner, DOWN)]))
                if last:
                    arrivals.append((both(has_down, near(d)), me + d, piece, [(near(-1), LEFT), (has_down, DOWN)]))
            for e in range(1, blocks):
                slot = me - e * columns
                sends = [(inner, DOWN)]
                if d == 0 and not last:
                    sends.append((near(-1), LEFT))
                if last:
                    sends.append((both(near(1), z == d), RIGHT))
                arrivals.append((both(x >= e, z >= d), slot - d, piece, sends))
                if d > 0:
                    sends = [(has_down, DOWN)] if last else [(near(-1), LEFT)]
                    arrivals.append((both(x >= e, near(d)), slot + d, piece, sends))

    def pending(e, c, piece):
        if e == 0:
            down = both(has_down, c > 0) if piece == LAST else has_down
            return both(c <= z, jnp.logical_not(both(c < z, either(near(1), down))))
        if piece == LAST:
            level = either(both(has_down, either(c > 0, z == 0)), both(c == 0, near(1)))
            passed = jnp.where(c <= z, one(level), one(has_down))
        else:
            passed = jnp.where(c <= z, one(either(has_down, both(c == z, near(-1)))), one(near(-1)))
        return both(x >= e, passed == 0)

    def passes(sends):
        needed = z < 0
        for condition, _ in sends:
            needed = either(needed, condition)
        return needed

    first_hops(lambda copy: copy.start())

    for slot in range(1, count):
        row, column = slot // columns, slot % columns
        later = both(x == row, z < column)

        @pl.when(either(x < row, later))
        def _():
            kv[slot, :, : LAST * width] = jnp.zeros((rows, LAST * width), kv.dtype)
            seg[slot] = jnp.zeros(seg.shape[1:], seg.dtype)

        @pl.when(either(x < row, both(later, jnp.logical_not(has_down))))
        def _():
            kv[slot, :, LAST * width :] = jnp.zeros((rows, width), kv.dtype)

    first_hops(lambda copy: copy.wait_send())
    own_hops(lambda copy: copy.start())
    query_copy.start()
    for valid, slot, piece, sends in arrivals:
        if sends:
            @pl.when(both(valid, passes(sends)))
            def _():
                wait_piece(slot, piece)
                for condition, way in sends:
                    @pl.when(condition)
                    def _():
                        for copy in copies(way, slot, piece, to[way]):
                            copy.start()

    query_heads = q.shape[1] // HEAD_SIZE
    key_heads = kv.shape[2] // (2 * HEAD_SIZE)
    group = query_heads // key_heads
    factor = math.log2(math.e) / math.sqrt(HEAD_SIZE)
    order = []
    for e in range(0, blocks, 2):
        for d in range(columns):
            pair = []
            for f in range(e, min(e + 2, blocks)):
                back, ahead = lax.rem(z - d + columns, columns), lax.rem(z + d, columns)
                c = back if f == 0 else jnp.where(2 * z < columns, ahead, back)
                pair.append((f, c, lax.rem(x - f + blocks, blocks) * columns + c))
            order.append(pair)

    query_copy.wait_recv()
    for n, pair in enumerate(order):
        for piece in range(PIECES):
            for e, c, slot in pair:
                @pl.when(pending(e, c, piece))
                def _():
                    wait_piece(slot, piece)
            if n == 0 and piece == 0:
                line = lax.broadcasted_iota(jnp.int32, (rows, rows), 0)
                lane = lax.broadcasted_iota(jnp.int32, (rows, rows), 1)
                own = jnp.broadcast_to(seg[me], (rows, rows))
                query_labels = jnp.sum(jnp.where(line == lane, own, 0), axis=1, keepdims=True)
            if piece == 0:
                biases = []
                for _, _, slot in pair:
                    allowed = both(slot * rows + lane <= me * rows + line, seg[slot] == query_labels)
                    biases.append(jnp.where(allowed, 0.0, MASKED))
                bias = jnp.concatenate(biases, axis=1)
                bias = jnp.concatenate([bias] * group, axis=0)
            for k in range(piece * key_heads // PIECES, (piece + 1) * key_heads // PIECES):
                at = 2 * k * HEAD_SIZE
                keys = jnp.concatenate([kv[slot, :, at : at + HEAD_SIZE] for _, _, slot in pair], axis=0)
                values = jnp.concatenate(
                    [kv[slot, :, at + HEAD_SIZE : at + 2 * HEAD_SIZE] for _, _, slot in pair], axis=0
                )
                queries = jnp.concatenate(
                    [q[:, h * HEAD_SIZE : (h + 1) * HEAD_SIZE] for h in range(group * k, group * (k + 1))], axis=0
                )
                scores = lax.dot_general(
                    queries, keys, (((1,), (1,)), ((), ())), preferred_element_type=jnp.float32
                ) + bias
                top = jnp.max(scores, axis=1, keepdims=True)
                if n > 0:
                    before_top = tops[k][:, :1]
                    top = jnp.maximum(before_top, top)
                weights = jnp.exp2((scores - top) * factor)
                mixed = jnp.dot(weights.astype(jnp.bfloat16), values, preferred_element_type=jnp.float32)
                if n > 0:
                    kept = jnp.exp2((before_top - top) * factor)
                    weights += totals[k] * kept
                    mixed += mixes[k] * kept
                if n < len(order) - 1:
                    tops[k] = jnp.broadcast_to(top, tops.shape[1:])
                    totals[k] = weights
                    mixes[k] = mixed
                else:
                    mixed = (mixed / jnp.sum(weights, axis=1, keepdims=True)).astype(jnp.bfloat16)
                    for g in range(group):
                        h = group * k + g
                        out_ref[0, :, h * HEAD_SIZE : (h + 1) * HEAD_SIZE] = mixed[g * rows : (g + 1) * rows]

    own_hops(lambda copy: copy.wait_send())
    query_copy.wait_send()
    for valid, slot, piece, sends in arrivals:
        for condition, way in sends:
            @pl.when(both(valid, condition))
            def _():
                for copy in copies(way, slot, piece, to[way]):
                    copy.wait_send()


def per_device(queries, keys_values, segment_ids):
    sections, blocks, columns = (lax.axis_size(a) for a in ("section", "blk", "head"))
    rows = queries.shape[1]
    count = blocks * columns
    key_heads = keys_values.shape[2] // (2 * HEAD_SIZE)
    stacked = rows * queries.shape[2] // HEAD_SIZE // key_heads
    queries, keys_values, segment_ids = (
        pltpu.with_memory_space_constraint(a, pltpu.HBM) for a in (queries, keys_values, segment_ids)
    )
    return pl.pallas_call(
        functools.partial(kernel, sections, blocks, columns),
        out_shape=jax.ShapeDtypeStruct(queries.shape, jnp.bfloat16),
        in_specs=[pl.BlockSpec(memory_space=pltpu.HBM)] * 3,
        out_specs=pl.BlockSpec(memory_space=pltpu.VMEM),
        scratch_shapes=[
            pltpu.VMEM(queries.shape[1:], jnp.bfloat16),
            pltpu.VMEM((count,) + keys_values.shape[1:], jnp.bfloat16),
            pltpu.VMEM((count, 1, rows), jnp.int32),
            pltpu.VMEM((key_heads, stacked, HEAD_SIZE), jnp.float32),
            pltpu.VMEM((key_heads, stacked, min(blocks, 2) * rows), jnp.float32),
            pltpu.VMEM((key_heads, stacked, HEAD_SIZE), jnp.float32),
            pltpu.SemaphoreType.DMA,
            pltpu.SemaphoreType.DMA,
            pltpu.SemaphoreType.DMA((4, count, PIECES)),
            pltpu.SemaphoreType.DMA((count, PIECES)),
            pltpu.SemaphoreType.DMA((4, count)),
            pltpu.SemaphoreType.DMA((count,)),
        ],
        compiler_params=pltpu.CompilerParams(
            collective_id=0, has_side_effects=True, vmem_limit_bytes=48 * 1024 * 1024
        ),
    )(queries, keys_values, segment_ids)


def solution(mesh):
    return jax.shard_map(
        per_device,
        mesh=mesh,
        in_specs=(
            P("section", ("blk", "head"), None),
            P("section", ("blk", "head"), None),
            P("section", ("blk", "head")),
        ),
        out_specs=P("section", ("blk", "head"), None),
        check_vma=False,
    )
```

```python
import functools
import math

import jax
import jax.numpy as jnp
from jax import lax
from jax.experimental import pallas as pl
from jax.experimental.pallas import tpu as pltpu
from jax.sharding import PartitionSpec as P

HEAD_SIZE = 128
MASKED = -1e30
MESH = pl.DeviceIdType.MESH
OWN, RIGHT, DOWN, LEFT = range(4)
PIECES = 2
LAST = PIECES - 1
BEHIND = 2


def kernel(
    sections, blocks, columns, q_in, kv_in, seg_in, out_ref,
    q, kv, seg, tops, totals, mixes, q_send, q_recv, kv_send, kv_recv, seg_send, seg_recv,
):
    s, x, z = lax.axis_index("section"), lax.axis_index("blk"), lax.axis_index("head")
    after, before = lax.rem(s + 1, sections), lax.rem(s + sections - 1, sections)
    rows = q.shape[0]
    me = x * columns + z
    count = blocks * columns
    has_down, has_up = x < blocks - 1, x > 0
    both, either = jnp.logical_and, jnp.logical_or
    near = lambda step: both(z + step >= 0, z + step < columns)

    barrier = pltpu.get_barrier_semaphore()

    def greet(condition, section, blk, head):
        @pl.when(condition)
        def _():
            pl.semaphore_signal(barrier, inc=1, device_id=(section, blk, head), device_id_type=MESH)

    greet(s >= 0, before, x, z)
    for section in (before, s):
        greet(has_up, section, x - 1, z)
        greet(near(-1), section, x, z - 1)
    greet(near(1), s, x, z + 1)
    greet(both(has_down, near(1)), before, x, z + 1)
    one = lambda condition: jnp.where(condition, 1, 0)
    targets = 1 + 2 * one(has_down) + 2 * one(near(1)) + one(near(-1)) + one(both(has_down, near(-1)))
    pl.semaphore_wait(barrier, targets)

    width = kv.shape[2] // PIECES

    def copies(way, slot, piece, device, first=False):
        part = pl.ds(piece * width, width)
        src = kv_in.at[0, :, part] if first else kv.at[slot, :, part]
        yield pltpu.make_async_remote_copy(
            src_ref=src, dst_ref=kv.at[slot, :, part], send_sem=kv_send.at[way, slot, piece],
            recv_sem=kv_recv.at[slot, piece], device_id=device, device_id_type=MESH,
        )
        if piece == 0:
            yield pltpu.make_async_remote_copy(
                src_ref=seg_in if first else seg.at[slot], dst_ref=seg.at[slot], send_sem=seg_send.at[way, slot],
                recv_sem=seg_recv.at[slot], device_id=device, device_id_type=MESH,
            )

    def wait_piece(slot, piece):
        for copy in copies(OWN, slot, piece, (after, x, z)):
            copy.wait_recv()

    query_copy = pltpu.make_async_remote_copy(
        src_ref=q_in.at[0], dst_ref=q, send_sem=q_send, recv_sem=q_recv,
        device_id=(after, x, z), device_id_type=MESH,
    )

    def own_hops(act):
        for piece in range(PIECES):
            for copy in copies(OWN, me, piece, (after, x, z), True):
                act(copy)

    def first_hops(act):
        for piece in range(PIECES):
            hops = [(near(1), RIGHT, (after, x, z + 1)), (has_down, DOWN, (after, x + 1, z))]
            if piece == LAST:
                hops.append((both(has_down, near(-1)), LEFT, (after, x, z - 1)))
            for condition, way, device in hops:
                @pl.when(condition)
                def _():
                    for copy in copies(way, me, piece, device, True):
                        act(copy)

    to = {RIGHT: (s, x, z + 1), DOWN: (s, x + 1, z), LEFT: (s, x, z - 1)}
    rounds = [[] for _ in range(columns)]
    for d, arrivals in enumerate(rounds):
        for piece in range(PIECES):
            last = piece == LAST
            inner = both(has_down, z > d) if last and d > 0 else has_down
            if d > 0:
                arrivals.append((z >= d, me - d, piece, [(near(1), RIGHT), (inner, DOWN)]))
                if last:
                    arrivals.append((both(has_down, near(d)), me + d, piece, [(near(-1), LEFT), (has_down, DOWN)]))
            for e in range(1, blocks):
                slot = me - e * columns
                sends = [(inner, DOWN)]
                if d == 0 and not last:
                    sends.append((near(-1), LEFT))
                if last:
                    sends.append((both(near(1), z == d), RIGHT))
                arrivals.append((both(x >= e, z >= d), slot - d, piece, sends))
                if d > 0:
                    sends = [(has_down, DOWN)] if last else [(near(-1), LEFT)]
                    arrivals.append((both(x >= e, near(d)), slot + d, piece, sends))

    def pending(e, c, piece):
        if e == 0:
            down = both(has_down, c > 0) if piece == LAST else has_down
            return both(c <= z, jnp.logical_not(both(c < z, either(near(1), down))))
        if piece == LAST:
            level = either(both(has_down, either(c > 0, z == 0)), both(c == 0, near(1)))
            passed = jnp.where(c <= z, one(level), one(has_down))
        else:
            passed = jnp.where(c <= z, one(either(has_down, both(c == z, near(-1)))), one(near(-1)))
        return both(x >= e, passed == 0)

    def passes(sends):
        needed = z < 0
        for condition, _ in sends:
            needed = either(needed, condition)
        return needed

    first_hops(lambda copy: copy.start())

    for slot in range(1, count):
        row, column = slot // columns, slot % columns
        later = both(x == row, z < column)

        @pl.when(either(x < row, later))
        def _():
            kv[slot, :, : LAST * width] = jnp.zeros((rows, LAST * width), kv.dtype)
            seg[slot] = jnp.zeros(seg.shape[1:], seg.dtype)

        @pl.when(either(x < row, both(later, jnp.logical_not(has_down))))
        def _():
            kv[slot, :, LAST * width :] = jnp.zeros((rows, width), kv.dtype)

    first_hops(lambda copy: copy.wait_send())
    own_hops(lambda copy: copy.start())
    query_copy.start()
    query_heads = q.shape[1] // HEAD_SIZE
    key_heads = kv.shape[2] // (2 * HEAD_SIZE)
    group = query_heads // key_heads
    factor = math.log2(math.e) / math.sqrt(HEAD_SIZE)
    order = []
    for e in range(0, blocks, 2):
        for d in range(columns):
            pair = []
            for f in range(e, min(e + 2, blocks)):
                back, ahead = lax.rem(z - d + columns, columns), lax.rem(z + d, columns)
                c = back if f == 0 else jnp.where(2 * z < columns, ahead, back)
                pair.append((f, c, lax.rem(x - f + blocks, blocks) * columns + c))
            needed = either(x >= e + 1, both(x >= e, z >= d if e == 0 else x >= e))
            order.append((needed, pair))

    line = lax.broadcasted_iota(jnp.int32, (rows, rows), 0)
    lane = lax.broadcasted_iota(jnp.int32, (rows, rows), 1)

    def attend(n):
        needed, pair = order[n]

        @pl.when(needed)
        def _():
            for piece in range(PIECES):
                for e, c, slot in pair:
                    @pl.when(pending(e, c, piece))
                    def _():
                        wait_piece(slot, piece)
                if piece == 0:
                    own = jnp.broadcast_to(seg[me], (rows, rows))
                    labels = jnp.sum(jnp.where(line == lane, own, 0), axis=1, keepdims=True)
                    biases = []
                    for _, _, slot in pair:
                        allowed = both(slot * rows + lane <= me * rows + line, seg[slot] == labels)
                        biases.append(jnp.where(allowed, 0.0, MASKED))
                    bias = jnp.concatenate(biases, axis=1)
                    bias = jnp.concatenate([bias] * group, axis=0)
                for k in range(piece * key_heads // PIECES, (piece + 1) * key_heads // PIECES):
                    at = 2 * k * HEAD_SIZE
                    keys = jnp.concatenate([kv[slot, :, at : at + HEAD_SIZE] for _, _, slot in pair], axis=0)
                    values = jnp.concatenate(
                        [kv[slot, :, at + HEAD_SIZE : at + 2 * HEAD_SIZE] for _, _, slot in pair], axis=0
                    )
                    heads = range(group * k, group * (k + 1))
                    queries = jnp.concatenate([q[:, h * HEAD_SIZE : (h + 1) * HEAD_SIZE] for h in heads], axis=0)
                    scores = lax.dot_general(
                        queries, keys, (((1,), (1,)), ((), ())), preferred_element_type=jnp.float32
                    ) + bias
                    top = jnp.broadcast_to(jnp.max(scores, axis=1, keepdims=True), scores.shape)
                    if n > 0:
                        before_top = tops[k]
                        top = jnp.maximum(before_top, top)
                    weights = jnp.exp2((scores - top) * factor)
                    mixed = jnp.dot(weights.astype(jnp.bfloat16), values, preferred_element_type=jnp.float32)
                    if n > 0:
                        kept = jnp.exp2((before_top - top) * factor)
                        weights += totals[k] * kept
                        mixed += mixes[k] * kept
                    tops[k] = top
                    totals[k] = weights
                    mixes[k] = mixed

    done = 0
    for d, arrivals in enumerate(rounds):
        for valid, slot, piece, sends in arrivals:
            @pl.when(both(valid, passes(sends)))
            def _():
                wait_piece(slot, piece)
                for condition, way in sends:
                    @pl.when(condition)
                    def _():
                        for copy in copies(way, slot, piece, to[way]):
                            copy.start()
        if blocks <= 2 and d >= BEHIND:
            if done == 0:
                query_copy.wait_recv()
            attend(done)
            done += 1
    if done == 0:
        query_copy.wait_recv()
    for n in range(done, len(order)):
        attend(n)
    for k in range(key_heads):
        mixed = (mixes[k] / jnp.sum(totals[k], axis=1, keepdims=True)).astype(jnp.bfloat16)
        for g in range(group):
            h = group * k + g
            out_ref[0, :, h * HEAD_SIZE : (h + 1) * HEAD_SIZE] = mixed[g * rows : (g + 1) * rows]

    own_hops(lambda copy: copy.wait_send())
    query_copy.wait_send()
    for valid, slot, piece, sends in sum(rounds, []):
        for condition, way in sends:
            @pl.when(both(valid, condition))
            def _():
                for copy in copies(way, slot, piece, to[way]):
                    copy.wait_send()


def per_device(queries, keys_values, segment_ids):
    sections, blocks, columns = (lax.axis_size(a) for a in ("section", "blk", "head"))
    rows = queries.shape[1]
    count = blocks * columns
    key_heads = keys_values.shape[2] // (2 * HEAD_SIZE)
    stacked = rows * queries.shape[2] // HEAD_SIZE // key_heads
    queries, keys_values, segment_ids = (
        pltpu.with_memory_space_constraint(a, pltpu.HBM) for a in (queries, keys_values, segment_ids)
    )
    return pl.pallas_call(
        functools.partial(kernel, sections, blocks, columns),
        out_shape=jax.ShapeDtypeStruct(queries.shape, jnp.bfloat16),
        in_specs=[pl.BlockSpec(memory_space=pltpu.HBM)] * 3,
        out_specs=pl.BlockSpec(memory_space=pltpu.VMEM),
        scratch_shapes=[
            pltpu.VMEM(queries.shape[1:], jnp.bfloat16),
            pltpu.VMEM((count,) + keys_values.shape[1:], jnp.bfloat16),
            pltpu.VMEM((count, 1, rows), jnp.int32),
            pltpu.VMEM((key_heads, stacked, min(blocks, 2) * rows), jnp.float32),
            pltpu.VMEM((key_heads, stacked, min(blocks, 2) * rows), jnp.float32),
            pltpu.VMEM((key_heads, stacked, HEAD_SIZE), jnp.float32),
            pltpu.SemaphoreType.DMA,
            pltpu.SemaphoreType.DMA,
            pltpu.SemaphoreType.DMA((4, count, PIECES)),
            pltpu.SemaphoreType.DMA((count, PIECES)),
            pltpu.SemaphoreType.DMA((4, count)),
            pltpu.SemaphoreType.DMA((count,)),
        ],
        compiler_params=pltpu.CompilerParams(
            collective_id=0, has_side_effects=True, vmem_limit_bytes=48 * 1024 * 1024
        ),
    )(queries, keys_values, segment_ids)


def solution(mesh):
    return jax.shard_map(
        per_device,
        mesh=mesh,
        in_specs=(
            P("section", ("blk", "head"), None),
            P("section", ("blk", "head"), None),
            P("section", ("blk", "head")),
        ),
        out_specs=P("section", ("blk", "head"), None),
        check_vma=False,
    )
```

```python
import functools
import math

import jax
import jax.numpy as jnp
from jax import lax
from jax.experimental import pallas as pl
from jax.experimental.pallas import tpu as pltpu
from jax.sharding import PartitionSpec as P

HEAD_SIZE = 128
MASKED = -1e30
MESH = pl.DeviceIdType.MESH
OWN, RIGHT, DOWN, LEFT = range(4)
PIECES = 2
LAST = PIECES - 1
BEHIND = 2


def kernel(
    sections, blocks, columns, q_in, kv_in, seg_in, out_ref,
    q, kv, seg, tops, totals, mixes, q_send, q_recv, kv_send, kv_recv, seg_send, seg_recv,
):
    s, x, z = lax.axis_index("section"), lax.axis_index("blk"), lax.axis_index("head")
    after, before = lax.rem(s + 1, sections), lax.rem(s + sections - 1, sections)
    rows = q.shape[0]
    me = x * columns + z
    count = blocks * columns
    has_down, has_up = x < blocks - 1, x > 0
    both, either = jnp.logical_and, jnp.logical_or
    near = lambda step: both(z + step >= 0, z + step < columns)

    barrier = pltpu.get_barrier_semaphore()

    def greet(condition, section, blk, head):
        @pl.when(condition)
        def _():
            pl.semaphore_signal(barrier, inc=1, device_id=(section, blk, head), device_id_type=MESH)

    greet(s >= 0, before, x, z)
    for section in (before, s):
        greet(has_up, section, x - 1, z)
        greet(near(-1), section, x, z - 1)
    greet(near(1), s, x, z + 1)
    greet(both(has_down, near(1)), before, x, z + 1)
    direct, relayed = lax.rem(s, 2) == 0, lax.rem(before, 2) == 1
    one = lambda condition: jnp.where(condition, 1, 0)
    targets = 1 + 2 * one(has_down) + 2 * one(near(1)) + one(near(-1)) + one(both(has_down, near(-1)))
    pl.semaphore_wait(barrier, targets)

    width = kv.shape[2] // PIECES

    def copies(way, slot, piece, device, first=False):
        part = pl.ds(piece * width, width)
        src = kv_in.at[0, :, part] if first else kv.at[slot, :, part]
        yield pltpu.make_async_remote_copy(
            src_ref=src, dst_ref=kv.at[slot, :, part], send_sem=kv_send.at[way, slot, piece],
            recv_sem=kv_recv.at[slot, piece], device_id=device, device_id_type=MESH,
        )
        if piece == 0:
            yield pltpu.make_async_remote_copy(
                src_ref=seg_in if first else seg.at[slot], dst_ref=seg.at[slot], send_sem=seg_send.at[way, slot],
                recv_sem=seg_recv.at[slot], device_id=device, device_id_type=MESH,
            )

    def wait_piece(slot, piece):
        for copy in copies(OWN, slot, piece, (after, x, z)):
            copy.wait_recv()

    query_copy = pltpu.make_async_remote_copy(
        src_ref=q_in.at[0], dst_ref=q, send_sem=q_send, recv_sem=q_recv,
        device_id=(after, x, z), device_id_type=MESH,
    )

    def own_hops(act):
        for piece in range(PIECES):
            for copy in copies(OWN, me, piece, (after, x, z), True):
                act(copy)

    def first_hops(act):
        for piece in range(PIECES):
            hops = [(near(1), RIGHT, (after, x, z + 1)), (has_down, DOWN, (after, x + 1, z))]
            if piece == LAST:
                hops.append((both(has_down, near(-1)), LEFT, (after, x, z - 1)))
            for condition, way, device in hops:
                @pl.when(both(direct, condition))
                def _():
                    for copy in copies(way, me, piece, device, True):
                        act(copy)

    to = {RIGHT: (s, x, z + 1), DOWN: (s, x + 1, z), LEFT: (s, x, z - 1)}
    rounds = [[] for _ in range(columns)]
    for d, arrivals in enumerate(rounds):
        for piece in range(PIECES):
            last = piece == LAST
            inner = both(has_down, z > d) if last and d > 0 else has_down
            if d == 0:
                sends = [(both(relayed, near(1)), RIGHT), (both(relayed, has_down), DOWN)]
                if last:
                    sends.append((both(relayed, both(has_down, near(-1))), LEFT))
                arrivals.append((z >= 0, me, piece, sends))
            else:
                arrivals.append((z >= d, me - d, piece, [(near(1), RIGHT), (inner, DOWN)]))
                if last:
                    arrivals.append((both(has_down, near(d)), me + d, piece, [(near(-1), LEFT), (has_down, DOWN)]))
            for e in range(1, blocks):
                slot = me - e * columns
                sends = [(inner, DOWN)]
                if d == 0 and not last:
                    sends.append((near(-1), LEFT))
                if last:
                    sends.append((both(near(1), z == d), RIGHT))
                arrivals.append((both(x >= e, z >= d), slot - d, piece, sends))
                if d > 0:
                    sends = [(has_down, DOWN)] if last else [(near(-1), LEFT)]
                    arrivals.append((both(x >= e, near(d)), slot + d, piece, sends))

    def pending(e, c, piece):
        if e == 0:
            down = both(has_down, c > 0) if piece == LAST else has_down
            passed = jnp.where(c < z, one(either(near(1), down)), one(both(relayed, either(near(1), has_down))))
            return both(c <= z, passed == 0)
        if piece == LAST:
            level = either(both(has_down, either(c > 0, z == 0)), both(c == 0, near(1)))
            passed = jnp.where(c <= z, one(level), one(has_down))
        else:
            passed = jnp.where(c <= z, one(either(has_down, both(c == z, near(-1)))), one(near(-1)))
        return both(x >= e, passed == 0)

    def passes(sends):
        needed = z < 0
        for condition, _ in sends:
            needed = either(needed, condition)
        return needed

    first_hops(lambda copy: copy.start())
    own_hops(lambda copy: copy.start())

    for slot in range(1, count):
        row, column = slot // columns, slot % columns
        later = both(x == row, z < column)

        @pl.when(either(x < row, later))
        def _():
            kv[slot, :, : LAST * width] = jnp.zeros((rows, LAST * width), kv.dtype)
            seg[slot] = jnp.zeros(seg.shape[1:], seg.dtype)

        @pl.when(either(x < row, both(later, jnp.logical_not(has_down))))
        def _():
            kv[slot, :, LAST * width :] = jnp.zeros((rows, width), kv.dtype)

    own_hops(lambda copy: copy.wait_send())
    query_copy.start()
    query_heads = q.shape[1] // HEAD_SIZE
    key_heads = kv.shape[2] // (2 * HEAD_SIZE)
    group = query_heads // key_heads
    factor = math.log2(math.e) / math.sqrt(HEAD_SIZE)
    order = []
    for e in range(0, blocks, 2):
        for d in range(columns):
            pair = []
            for f in range(e, min(e + 2, blocks)):
                back, ahead = lax.rem(z - d + columns, columns), lax.rem(z + d, columns)
                c = back if f == 0 else jnp.where(2 * z < columns, ahead, back)
                pair.append((f, c, lax.rem(x - f + blocks, blocks) * columns + c))
            needed = either(x >= e + 1, both(x >= e, z >= d if e == 0 else x >= e))
            order.append((needed, pair))

    line = lax.broadcasted_iota(jnp.int32, (rows, rows), 0)
    lane = lax.broadcasted_iota(jnp.int32, (rows, rows), 1)

    def attend(n):
        needed, pair = order[n]

        @pl.when(needed)
        def _():
            for piece in range(PIECES):
                for e, c, slot in pair:
                    @pl.when(pending(e, c, piece))
                    def _():
                        wait_piece(slot, piece)
                if piece == 0:
                    own = jnp.broadcast_to(seg[me], (rows, rows))
                    labels = jnp.sum(jnp.where(line == lane, own, 0), axis=1, keepdims=True)
                    biases = []
                    for _, _, slot in pair:
                        allowed = both(slot * rows + lane <= me * rows + line, seg[slot] == labels)
                        biases.append(jnp.where(allowed, 0.0, MASKED))
                    bias = jnp.concatenate(biases, axis=1)
                    bias = jnp.concatenate([bias] * group, axis=0)
                for k in range(piece * key_heads // PIECES, (piece + 1) * key_heads // PIECES):
                    at = 2 * k * HEAD_SIZE
                    keys = jnp.concatenate([kv[slot, :, at : at + HEAD_SIZE] for _, _, slot in pair], axis=0)
                    values = jnp.concatenate(
                        [kv[slot, :, at + HEAD_SIZE : at + 2 * HEAD_SIZE] for _, _, slot in pair], axis=0
                    )
                    heads = range(group * k, group * (k + 1))
                    queries = jnp.concatenate([q[:, h * HEAD_SIZE : (h + 1) * HEAD_SIZE] for h in heads], axis=0)
                    scores = lax.dot_general(
                        queries, keys, (((1,), (1,)), ((), ())), preferred_element_type=jnp.float32
                    ) + bias
                    top = jnp.broadcast_to(jnp.max(scores, axis=1, keepdims=True), scores.shape)
                    if n > 0:
                        before_top = tops[k]
                        top = jnp.maximum(before_top, top)
                    weights = jnp.exp2((scores - top) * factor)
                    mixed = jnp.dot(weights.astype(jnp.bfloat16), values, preferred_element_type=jnp.float32)
                    if n > 0:
                        kept = jnp.exp2((before_top - top) * factor)
                        weights += totals[k] * kept
                        mixed += mixes[k] * kept
                    tops[k] = top
                    totals[k] = weights
                    mixes[k] = mixed

    done = 0
    for d, arrivals in enumerate(rounds):
        for valid, slot, piece, sends in arrivals:
            @pl.when(both(valid, passes(sends)))
            def _():
                wait_piece(slot, piece)
                for condition, way in sends:
                    @pl.when(condition)
                    def _():
                        for copy in copies(way, slot, piece, to[way]):
                            copy.start()
        if blocks <= 2 and d >= BEHIND:
            if done == 0:
                query_copy.wait_recv()
            attend(done)
            done += 1
    if done == 0:
        query_copy.wait_recv()
    for n in range(done, len(order)):
        attend(n)
    for k in range(key_heads):
        mixed = (mixes[k] / jnp.sum(totals[k], axis=1, keepdims=True)).astype(jnp.bfloat16)
        for g in range(group):
            h = group * k + g
            out_ref[0, :, h * HEAD_SIZE : (h + 1) * HEAD_SIZE] = mixed[g * rows : (g + 1) * rows]

    first_hops(lambda copy: copy.wait_send())
    query_copy.wait_send()
    for valid, slot, piece, sends in sum(rounds, []):
        for condition, way in sends:
            @pl.when(both(valid, condition))
            def _():
                for copy in copies(way, slot, piece, to[way]):
                    copy.wait_send()


def per_device(queries, keys_values, segment_ids):
    sections, blocks, columns = (lax.axis_size(a) for a in ("section", "blk", "head"))
    rows = queries.shape[1]
    count = blocks * columns
    key_heads = keys_values.shape[2] // (2 * HEAD_SIZE)
    stacked = rows * queries.shape[2] // HEAD_SIZE // key_heads
    queries, keys_values, segment_ids = (
        pltpu.with_memory_space_constraint(a, pltpu.HBM) for a in (queries, keys_values, segment_ids)
    )
    return pl.pallas_call(
        functools.partial(kernel, sections, blocks, columns),
        out_shape=jax.ShapeDtypeStruct(queries.shape, jnp.bfloat16),
        in_specs=[pl.BlockSpec(memory_space=pltpu.HBM)] * 3,
        out_specs=pl.BlockSpec(memory_space=pltpu.VMEM),
        scratch_shapes=[
            pltpu.VMEM(queries.shape[1:], jnp.bfloat16),
            pltpu.VMEM((count,) + keys_values.shape[1:], jnp.bfloat16),
            pltpu.VMEM((count, 1, rows), jnp.int32),
            pltpu.VMEM((key_heads, stacked, min(blocks, 2) * rows), jnp.float32),
            pltpu.VMEM((key_heads, stacked, min(blocks, 2) * rows), jnp.float32),
            pltpu.VMEM((key_heads, stacked, HEAD_SIZE), jnp.float32),
            pltpu.SemaphoreType.DMA,
            pltpu.SemaphoreType.DMA,
            pltpu.SemaphoreType.DMA((4, count, PIECES)),
            pltpu.SemaphoreType.DMA((count, PIECES)),
            pltpu.SemaphoreType.DMA((4, count)),
            pltpu.SemaphoreType.DMA((count,)),
        ],
        compiler_params=pltpu.CompilerParams(
            collective_id=0, has_side_effects=True, vmem_limit_bytes=48 * 1024 * 1024
        ),
    )(queries, keys_values, segment_ids)


def solution(mesh):
    return jax.shard_map(
        per_device,
        mesh=mesh,
        in_specs=(
            P("section", ("blk", "head"), None),
            P("section", ("blk", "head"), None),
            P("section", ("blk", "head")),
        ),
        out_specs=P("section", ("blk", "head"), None),
        check_vma=False,
    )
```

```python
import functools
import math

import jax
import jax.numpy as jnp
from jax import lax
from jax.experimental import pallas as pl
from jax.experimental.pallas import tpu as pltpu
from jax.sharding import PartitionSpec as P

HEAD_SIZE = 128
MASKED = -1e30
MESH = pl.DeviceIdType.MESH
OWN, RIGHT, DOWN, LEFT = range(4)
PIECES = 2
LAST = PIECES - 1
BEHIND = 1


def kernel(
    sections, blocks, columns, q_in, kv_in, seg_in, out_ref,
    q, kv, seg, tops, totals, mixes, q_send, q_recv, kv_send, kv_recv, seg_send, seg_recv,
):
    s, x, z = lax.axis_index("section"), lax.axis_index("blk"), lax.axis_index("head")
    after, before = lax.rem(s + 1, sections), lax.rem(s + sections - 1, sections)
    rows = q.shape[0]
    me = x * columns + z
    count = blocks * columns
    has_down, has_up = x < blocks - 1, x > 0
    both, either = jnp.logical_and, jnp.logical_or
    near = lambda step: both(z + step >= 0, z + step < columns)

    barrier = pltpu.get_barrier_semaphore()

    def greet(condition, section, blk, head):
        @pl.when(condition)
        def _():
            pl.semaphore_signal(barrier, inc=1, device_id=(section, blk, head), device_id_type=MESH)

    greet(s >= 0, before, x, z)
    for section in (before, s):
        greet(has_up, section, x - 1, z)
        greet(near(-1), section, x, z - 1)
    greet(near(1), s, x, z + 1)
    greet(both(has_down, near(1)), before, x, z + 1)
    one = lambda condition: jnp.where(condition, 1, 0)
    targets = 1 + 2 * one(has_down) + 2 * one(near(1)) + one(near(-1)) + one(both(has_down, near(-1)))
    pl.semaphore_wait(barrier, targets)

    width = kv.shape[2] // PIECES

    def copies(way, slot, piece, device, first=False):
        part = pl.ds(piece * width, width)
        src = kv_in.at[0, :, part] if first else kv.at[slot, :, part]
        yield pltpu.make_async_remote_copy(
            src_ref=src, dst_ref=kv.at[slot, :, part], send_sem=kv_send.at[way, slot, piece],
            recv_sem=kv_recv.at[slot, piece], device_id=device, device_id_type=MESH,
        )
        if piece == 0:
            yield pltpu.make_async_remote_copy(
                src_ref=seg_in if first else seg.at[slot], dst_ref=seg.at[slot], send_sem=seg_send.at[way, slot],
                recv_sem=seg_recv.at[slot], device_id=device, device_id_type=MESH,
            )

    def wait_piece(slot, piece):
        for copy in copies(OWN, slot, piece, (after, x, z)):
            copy.wait_recv()

    query_copy = pltpu.make_async_remote_copy(
        src_ref=q_in.at[0], dst_ref=q, send_sem=q_send, recv_sem=q_recv,
        device_id=(after, x, z), device_id_type=MESH,
    )

    def own_hops(act):
        for piece in range(PIECES):
            for copy in copies(OWN, me, piece, (after, x, z), True):
                act(copy)

    def first_hops(act):
        for piece in range(PIECES):
            hops = [(near(1), RIGHT, (after, x, z + 1)), (has_down, DOWN, (after, x + 1, z))]
            if piece == LAST:
                hops.append((both(has_down, near(-1)), LEFT, (after, x, z - 1)))
            for condition, way, device in hops:
                @pl.when(condition)
                def _():
                    for copy in copies(way, me, piece, device, True):
                        act(copy)

    to = {RIGHT: (s, x, z + 1), DOWN: (s, x + 1, z), LEFT: (s, x, z - 1)}
    rounds = [[] for _ in range(columns)]
    for d, arrivals in enumerate(rounds):
        for piece in range(PIECES):
            last = piece == LAST
            inner = both(has_down, z > d) if last and d > 0 else has_down
            if d > 0:
                arrivals.append((z >= d, me - d, piece, [(near(1), RIGHT), (inner, DOWN)]))
                if last:
                    arrivals.append((both(has_down, near(d)), me + d, piece, [(near(-1), LEFT), (has_down, DOWN)]))
            for e in range(1, blocks):
                slot = me - e * columns
                sends = [(inner, DOWN)]
                if d == 0 and not last:
                    sends.append((near(-1), LEFT))
                if last:
                    sends.append((both(near(1), z == d), RIGHT))
                arrivals.append((both(x >= e, z >= d), slot - d, piece, sends))
                if d > 0:
                    sends = [(has_down, DOWN)] if last else [(near(-1), LEFT)]
                    arrivals.append((both(x >= e, near(d)), slot + d, piece, sends))

    def pending(e, c, piece):
        if e == 0:
            down = both(has_down, c > 0) if piece == LAST else has_down
            return both(c <= z, jnp.logical_not(both(c < z, either(near(1), down))))
        if piece == LAST:
            level = either(both(has_down, either(c > 0, z == 0)), both(c == 0, near(1)))
            passed = jnp.where(c <= z, one(level), one(has_down))
        else:
            passed = jnp.where(c <= z, one(either(has_down, both(c == z, near(-1)))), one(near(-1)))
        return both(x >= e, passed == 0)

    def passes(sends):
        needed = z < 0
        for condition, _ in sends:
            needed = either(needed, condition)
        return needed

    first_hops(lambda copy: copy.start())
    own_hops(lambda copy: copy.start())

    for slot in range(1, count):
        row, column = slot // columns, slot % columns
        later = both(x == row, z < column)

        @pl.when(either(x < row, later))
        def _():
            kv[slot, :, : LAST * width] = jnp.zeros((rows, LAST * width), kv.dtype)
            seg[slot] = jnp.zeros(seg.shape[1:], seg.dtype)

        @pl.when(either(x < row, both(later, jnp.logical_not(has_down))))
        def _():
            kv[slot, :, LAST * width :] = jnp.zeros((rows, width), kv.dtype)

    own_hops(lambda copy: copy.wait_send())
    query_copy.start()
    query_heads = q.shape[1] // HEAD_SIZE
    key_heads = kv.shape[2] // (2 * HEAD_SIZE)
    group = query_heads // key_heads
    factor = math.log2(math.e) / math.sqrt(HEAD_SIZE)
    order = []
    for e in range(0, blocks, 2):
        for d in range(columns):
            pair = []
            for f in range(e, min(e + 2, blocks)):
                back, ahead = lax.rem(z - d + columns, columns), lax.rem(z + d, columns)
                c = back if f == 0 else jnp.where(2 * z < columns, ahead, back)
                pair.append((f, c, lax.rem(x - f + blocks, blocks) * columns + c))
            needed = either(x >= e + 1, both(x >= e, z >= d if e == 0 else x >= e))
            order.append((needed, pair))

    line = lax.broadcasted_iota(jnp.int32, (rows, rows), 0)
    lane = lax.broadcasted_iota(jnp.int32, (rows, rows), 1)

    def attend(n):
        needed, pair = order[n]

        @pl.when(needed)
        def _():
            for piece in range(PIECES):
                for e, c, slot in pair:
                    @pl.when(pending(e, c, piece))
                    def _():
                        wait_piece(slot, piece)
                if piece == 0:
                    own = jnp.broadcast_to(seg[me], (rows, rows))
                    labels = jnp.sum(jnp.where(line == lane, own, 0), axis=1, keepdims=True)
                    biases = []
                    for _, _, slot in pair:
                        allowed = both(slot * rows + lane <= me * rows + line, seg[slot] == labels)
                        biases.append(jnp.where(allowed, 0.0, MASKED))
                    bias = jnp.concatenate(biases, axis=1)
                    bias = jnp.concatenate([bias] * group, axis=0)
                for k in range(piece * key_heads // PIECES, (piece + 1) * key_heads // PIECES):
                    at = 2 * k * HEAD_SIZE
                    keys = jnp.concatenate([kv[slot, :, at : at + HEAD_SIZE] for _, _, slot in pair], axis=0)
                    values = jnp.concatenate(
                        [kv[slot, :, at + HEAD_SIZE : at + 2 * HEAD_SIZE] for _, _, slot in pair], axis=0
                    )
                    heads = range(group * k, group * (k + 1))
                    queries = jnp.concatenate([q[:, h * HEAD_SIZE : (h + 1) * HEAD_SIZE] for h in heads], axis=0)
                    scores = lax.dot_general(
                        queries, keys, (((1,), (1,)), ((), ())), preferred_element_type=jnp.float32
                    ) + bias
                    top = jnp.broadcast_to(jnp.max(scores, axis=1, keepdims=True), scores.shape)
                    if n > 0:
                        before_top = tops[k]
                        top = jnp.maximum(before_top, top)
                    weights = jnp.exp2((scores - top) * factor)
                    mixed = jnp.dot(weights.astype(jnp.bfloat16), values, preferred_element_type=jnp.float32)
                    if n > 0:
                        kept = jnp.exp2((before_top - top) * factor)
                        weights += totals[k] * kept
                        mixed += mixes[k] * kept
                    tops[k] = top
                    totals[k] = weights
                    mixes[k] = mixed

    done = 0
    for d, arrivals in enumerate(rounds):
        for valid, slot, piece, sends in arrivals:
            @pl.when(both(valid, passes(sends)))
            def _():
                wait_piece(slot, piece)
                for condition, way in sends:
                    @pl.when(condition)
                    def _():
                        for copy in copies(way, slot, piece, to[way]):
                            copy.start()
        if blocks <= 2 and d >= BEHIND:
            if done == 0:
                query_copy.wait_recv()
            attend(done)
            done += 1
    if done == 0:
        query_copy.wait_recv()
    for n in range(done, len(order)):
        attend(n)
    for k in range(key_heads):
        mixed = (mixes[k] / jnp.sum(totals[k], axis=1, keepdims=True)).astype(jnp.bfloat16)
        for g in range(group):
            h = group * k + g
            out_ref[0, :, h * HEAD_SIZE : (h + 1) * HEAD_SIZE] = mixed[g * rows : (g + 1) * rows]

    first_hops(lambda copy: copy.wait_send())
    query_copy.wait_send()
    for valid, slot, piece, sends in sum(rounds, []):
        for condition, way in sends:
            @pl.when(both(valid, condition))
            def _():
                for copy in copies(way, slot, piece, to[way]):
                    copy.wait_send()


def per_device(queries, keys_values, segment_ids):
    sections, blocks, columns = (lax.axis_size(a) for a in ("section", "blk", "head"))
    rows = queries.shape[1]
    count = blocks * columns
    key_heads = keys_values.shape[2] // (2 * HEAD_SIZE)
    stacked = rows * queries.shape[2] // HEAD_SIZE // key_heads
    queries, keys_values, segment_ids = (
        pltpu.with_memory_space_constraint(a, pltpu.HBM) for a in (queries, keys_values, segment_ids)
    )
    return pl.pallas_call(
        functools.partial(kernel, sections, blocks, columns),
        out_shape=jax.ShapeDtypeStruct(queries.shape, jnp.bfloat16),
        in_specs=[pl.BlockSpec(memory_space=pltpu.HBM)] * 3,
        out_specs=pl.BlockSpec(memory_space=pltpu.VMEM),
        scratch_shapes=[
            pltpu.VMEM(queries.shape[1:], jnp.bfloat16),
            pltpu.VMEM((count,) + keys_values.shape[1:], jnp.bfloat16),
            pltpu.VMEM((count, 1, rows), jnp.int32),
            pltpu.VMEM((key_heads, stacked, min(blocks, 2) * rows), jnp.float32),
            pltpu.VMEM((key_heads, stacked, min(blocks, 2) * rows), jnp.float32),
            pltpu.VMEM((key_heads, stacked, HEAD_SIZE), jnp.float32),
            pltpu.SemaphoreType.DMA,
            pltpu.SemaphoreType.DMA,
            pltpu.SemaphoreType.DMA((4, count, PIECES)),
            pltpu.SemaphoreType.DMA((count, PIECES)),
            pltpu.SemaphoreType.DMA((4, count)),
            pltpu.SemaphoreType.DMA((count,)),
        ],
        compiler_params=pltpu.CompilerParams(
            collective_id=0, has_side_effects=True, vmem_limit_bytes=48 * 1024 * 1024
        ),
    )(queries, keys_values, segment_ids)


def solution(mesh):
    return jax.shard_map(
        per_device,
        mesh=mesh,
        in_specs=(
            P("section", ("blk", "head"), None),
            P("section", ("blk", "head"), None),
            P("section", ("blk", "head")),
        ),
        out_specs=P("section", ("blk", "head"), None),
        check_vma=False,
    )
```

```python
import functools
import math

import jax
import jax.numpy as jnp
from jax import lax
from jax.experimental import pallas as pl
from jax.experimental.pallas import tpu as pltpu
from jax.sharding import PartitionSpec as P

HEAD_SIZE = 128
MASKED = -1e30
MESH = pl.DeviceIdType.MESH
OWN, RIGHT, DOWN, LEFT = range(4)
PIECES = 2
LAST = PIECES - 1


def kernel(
    sections, blocks, columns, q_in, kv_in, seg_in, out_ref,
    q, kv, seg, tops, totals, mixes, q_send, q_recv, kv_send, kv_recv, seg_send, seg_recv,
):
    s, x, z = lax.axis_index("section"), lax.axis_index("blk"), lax.axis_index("head")
    after, before = lax.rem(s + 1, sections), lax.rem(s + sections - 1, sections)
    rows = q.shape[0]
    me = x * columns + z
    count = blocks * columns
    has_down, has_up = x < blocks - 1, x > 0
    both, either = jnp.logical_and, jnp.logical_or
    near = lambda step: both(z + step >= 0, z + step < columns)

    barrier = pltpu.get_barrier_semaphore()

    def greet(condition, section, blk, head):
        @pl.when(condition)
        def _():
            pl.semaphore_signal(barrier, inc=1, device_id=(section, blk, head), device_id_type=MESH)

    greet(s >= 0, before, x, z)
    for section in (before, s):
        greet(has_up, section, x - 1, z)
        greet(near(-1), section, x, z - 1)
    greet(near(1), s, x, z + 1)
    greet(both(has_down, near(1)), before, x, z + 1)
    one = lambda condition: jnp.where(condition, 1, 0)
    targets = 1 + 2 * one(has_down) + 2 * one(near(1)) + one(near(-1)) + one(both(has_down, near(-1)))
    pl.semaphore_wait(barrier, targets)

    width = kv.shape[2] // PIECES

    def copies(way, slot, piece, device, first=False):
        part = pl.ds(piece * width, width)
        src = kv_in.at[0, :, part] if first else kv.at[slot, :, part]
        yield pltpu.make_async_remote_copy(
            src_ref=src, dst_ref=kv.at[slot, :, part], send_sem=kv_send.at[way, slot, piece],
            recv_sem=kv_recv.at[slot, piece], device_id=device, device_id_type=MESH,
        )
        if piece == 0:
            yield pltpu.make_async_remote_copy(
                src_ref=seg_in if first else seg.at[slot], dst_ref=seg.at[slot], send_sem=seg_send.at[way, slot],
                recv_sem=seg_recv.at[slot], device_id=device, device_id_type=MESH,
            )

    def wait_piece(slot, piece):
        for copy in copies(OWN, slot, piece, (after, x, z)):
            copy.wait_recv()

    query_copy = pltpu.make_async_remote_copy(
        src_ref=q_in.at[0], dst_ref=q, send_sem=q_send, recv_sem=q_recv,
        device_id=(after, x, z), device_id_type=MESH,
    )

    def own_hops(act):
        for piece in range(PIECES):
            for copy in copies(OWN, me, piece, (after, x, z), True):
                act(copy)

    def first_hops(act):
        for piece in range(PIECES):
            hops = [(near(1), RIGHT, (after, x, z + 1)), (has_down, DOWN, (after, x + 1, z))]
            if piece == LAST:
                hops.append((both(has_down, near(-1)), LEFT, (after, x, z - 1)))
            for condition, way, device in hops:
                @pl.when(condition)
                def _():
                    for copy in copies(way, me, piece, device, True):
                        act(copy)

    to = {RIGHT: (s, x, z + 1), DOWN: (s, x + 1, z), LEFT: (s, x, z - 1)}
    rounds = [[] for _ in range(columns)]
    for d, arrivals in enumerate(rounds):
        for piece in range(PIECES):
            last = piece == LAST
            inner = both(has_down, z > d) if last and d > 0 else has_down
            if d > 0:
                arrivals.append((z >= d, me - d, piece, [(near(1), RIGHT), (inner, DOWN)]))
                if last:
                    arrivals.append((both(has_down, near(d)), me + d, piece, [(near(-1), LEFT), (has_down, DOWN)]))
            for e in range(1, blocks):
                slot = me - e * columns
                sends = [(inner, DOWN)]
                if d == 0 and not last:
                    sends.append((near(-1), LEFT))
                if last:
                    sends.append((both(near(1), z == d), RIGHT))
                arrivals.append((both(x >= e, z >= d), slot - d, piece, sends))
                if d > 0:
                    sends = [(has_down, DOWN)] if last else [(near(-1), LEFT)]
                    arrivals.append((both(x >= e, near(d)), slot + d, piece, sends))

    def pending(e, c, piece):
        if e == 0:
            down = both(has_down, c > 0) if piece == LAST else has_down
            return both(c <= z, jnp.logical_not(both(c < z, either(near(1), down))))
        if piece == LAST:
            level = either(both(has_down, either(c > 0, z == 0)), both(c == 0, near(1)))
            passed = jnp.where(c <= z, one(level), one(has_down))
        else:
            passed = jnp.where(c <= z, one(either(has_down, both(c == z, near(-1)))), one(near(-1)))
        return both(x >= e, passed == 0)

    def passes(sends):
        needed = z < 0
        for condition, _ in sends:
            needed = either(needed, condition)
        return needed

    same_chip = lax.rem(s, 2) == 0

    def last_hops():
        own_hops(lambda copy: copy.start())
        query_copy.start()

    first_hops(lambda copy: copy.start())
    pl.when(same_chip)(last_hops)

    for slot in range(1, count):
        row, column = slot // columns, slot % columns
        later = both(x == row, z < column)

        @pl.when(either(x < row, later))
        def _():
            kv[slot, :, : LAST * width] = jnp.zeros((rows, LAST * width), kv.dtype)
            seg[slot] = jnp.zeros(seg.shape[1:], seg.dtype)

        @pl.when(either(x < row, both(later, jnp.logical_not(has_down))))
        def _():
            kv[slot, :, LAST * width :] = jnp.zeros((rows, width), kv.dtype)

    @pl.when(jnp.logical_not(same_chip))
    def _():
        first_hops(lambda copy: copy.wait_send())
        last_hops()

    query_heads = q.shape[1] // HEAD_SIZE
    key_heads = kv.shape[2] // (2 * HEAD_SIZE)
    group = query_heads // key_heads
    factor = math.log2(math.e) / math.sqrt(HEAD_SIZE)
    order = []
    for e in range(0, blocks, 2):
        for d in range(columns):
            pair = []
            for f in range(e, min(e + 2, blocks)):
                back, ahead = lax.rem(z - d + columns, columns), lax.rem(z + d, columns)
                c = back if f == 0 else jnp.where(2 * z < columns, ahead, back)
                pair.append((f, c, lax.rem(x - f + blocks, blocks) * columns + c))
            needed = either(x >= e + 1, both(x >= e, z >= d if e == 0 else x >= e))
            order.append((needed, pair))

    line = lax.broadcasted_iota(jnp.int32, (rows, rows), 0)
    lane = lax.broadcasted_iota(jnp.int32, (rows, rows), 1)

    def attend(n):
        needed, pair = order[n]

        @pl.when(needed)
        def _():
            for piece in range(PIECES):
                for e, c, slot in pair:
                    @pl.when(pending(e, c, piece))
                    def _():
                        wait_piece(slot, piece)
                if piece == 0:
                    own = jnp.broadcast_to(seg[me], (rows, rows))
                    labels = jnp.sum(jnp.where(line == lane, own, 0), axis=1, keepdims=True)
                    biases = []
                    for _, _, slot in pair:
                        allowed = both(slot * rows + lane <= me * rows + line, seg[slot] == labels)
                        biases.append(jnp.where(allowed, 0.0, MASKED))
                    bias = jnp.concatenate(biases, axis=1)
                    bias = jnp.concatenate([bias] * group, axis=0)
                for k in range(piece * key_heads // PIECES, (piece + 1) * key_heads // PIECES):
                    at = 2 * k * HEAD_SIZE
                    keys = jnp.concatenate([kv[slot, :, at : at + HEAD_SIZE] for _, _, slot in pair], axis=0)
                    values = jnp.concatenate(
                        [kv[slot, :, at + HEAD_SIZE : at + 2 * HEAD_SIZE] for _, _, slot in pair], axis=0
                    )
                    heads = range(group * k, group * (k + 1))
                    queries = jnp.concatenate([q[:, h * HEAD_SIZE : (h + 1) * HEAD_SIZE] for h in heads], axis=0)
                    scores = lax.dot_general(
                        queries, keys, (((1,), (1,)), ((), ())), preferred_element_type=jnp.float32
                    ) + bias
                    top = jnp.broadcast_to(jnp.max(scores, axis=1, keepdims=True), scores.shape)
                    if n > 0:
                        before_top = tops[k]
                        top = jnp.maximum(before_top, top)
                    weights = jnp.exp2((scores - top) * factor)
                    mixed = jnp.dot(weights.astype(jnp.bfloat16), values, preferred_element_type=jnp.float32)
                    if n > 0:
                        kept = jnp.exp2((before_top - top) * factor)
                        weights += totals[k] * kept
                        mixed += mixes[k] * kept
                    tops[k] = top
                    totals[k] = weights
                    mixes[k] = mixed

    for arrivals in rounds:
        for valid, slot, piece, sends in arrivals:
            @pl.when(both(valid, passes(sends)))
            def _():
                wait_piece(slot, piece)
                for condition, way in sends:
                    @pl.when(condition)
                    def _():
                        for copy in copies(way, slot, piece, to[way]):
                            copy.start()
    query_copy.wait_recv()
    for n in range(len(order)):
        attend(n)
    for k in range(key_heads):
        mixed = (mixes[k] / jnp.sum(totals[k], axis=1, keepdims=True)).astype(jnp.bfloat16)
        for g in range(group):
            h = group * k + g
            out_ref[0, :, h * HEAD_SIZE : (h + 1) * HEAD_SIZE] = mixed[g * rows : (g + 1) * rows]

    @pl.when(same_chip)
    def _():
        first_hops(lambda copy: copy.wait_send())

    own_hops(lambda copy: copy.wait_send())
    query_copy.wait_send()
    for valid, slot, piece, sends in sum(rounds, []):
        for condition, way in sends:
            @pl.when(both(valid, condition))
            def _():
                for copy in copies(way, slot, piece, to[way]):
                    copy.wait_send()


def per_device(queries, keys_values, segment_ids):
    sections, blocks, columns = (lax.axis_size(a) for a in ("section", "blk", "head"))
    rows = queries.shape[1]
    count = blocks * columns
    key_heads = keys_values.shape[2] // (2 * HEAD_SIZE)
    stacked = rows * queries.shape[2] // HEAD_SIZE // key_heads
    queries, keys_values, segment_ids = (
        pltpu.with_memory_space_constraint(a, pltpu.HBM) for a in (queries, keys_values, segment_ids)
    )
    return pl.pallas_call(
        functools.partial(kernel, sections, blocks, columns),
        out_shape=jax.ShapeDtypeStruct(queries.shape, jnp.bfloat16),
        in_specs=[pl.BlockSpec(memory_space=pltpu.HBM)] * 3,
        out_specs=pl.BlockSpec(memory_space=pltpu.VMEM),
        scratch_shapes=[
            pltpu.VMEM(queries.shape[1:], jnp.bfloat16),
            pltpu.VMEM((count,) + keys_values.shape[1:], jnp.bfloat16),
            pltpu.VMEM((count, 1, rows), jnp.int32),
            pltpu.VMEM((key_heads, stacked, min(blocks, 2) * rows), jnp.float32),
            pltpu.VMEM((key_heads, stacked, min(blocks, 2) * rows), jnp.float32),
            pltpu.VMEM((key_heads, stacked, HEAD_SIZE), jnp.float32),
            pltpu.SemaphoreType.DMA,
            pltpu.SemaphoreType.DMA,
            pltpu.SemaphoreType.DMA((4, count, PIECES)),
            pltpu.SemaphoreType.DMA((count, PIECES)),
            pltpu.SemaphoreType.DMA((4, count)),
            pltpu.SemaphoreType.DMA((count,)),
        ],
        compiler_params=pltpu.CompilerParams(
            collective_id=0, has_side_effects=True, vmem_limit_bytes=48 * 1024 * 1024
        ),
    )(queries, keys_values, segment_ids)


def solution(mesh):
    return jax.shard_map(
        per_device,
        mesh=mesh,
        in_specs=(
            P("section", ("blk", "head"), None),
            P("section", ("blk", "head"), None),
            P("section", ("blk", "head")),
        ),
        out_specs=P("section", ("blk", "head"), None),
        check_vma=False,
    )
```

```python
import functools
import math

import jax
import jax.numpy as jnp
from jax import lax
from jax.experimental import pallas as pl
from jax.experimental.pallas import tpu as pltpu
from jax.sharding import PartitionSpec as P

HEAD_SIZE = 128
MASKED = -1e30
MESH = pl.DeviceIdType.MESH
OWN, RIGHT, DOWN, LEFT, DIAGONAL = range(5)
PIECES = 2
LAST = PIECES - 1


def kernel(
    sections, blocks, columns, q_in, kv_in, seg_in, out_ref,
    q, kv, seg, tops, totals, mixes, q_send, q_recv, kv_send, kv_recv, seg_send, seg_recv,
):
    s, x, z = lax.axis_index("section"), lax.axis_index("blk"), lax.axis_index("head")
    after, before = lax.rem(s + 1, sections), lax.rem(s + sections - 1, sections)
    rows = q.shape[0]
    me = x * columns + z
    count = blocks * columns
    has_down, has_up = x < blocks - 1, x > 0
    both, either = jnp.logical_and, jnp.logical_or
    near = lambda step: both(z + step >= 0, z + step < columns)

    barrier = pltpu.get_barrier_semaphore()

    def greet(condition, section, blk, head):
        @pl.when(condition)
        def _():
            pl.semaphore_signal(barrier, inc=1, device_id=(section, blk, head), device_id_type=MESH)

    greet(s >= 0, before, x, z)
    for section in (before, s):
        greet(has_up, section, x - 1, z)
        greet(near(-1), section, x, z - 1)
    greet(near(1), s, x, z + 1)
    greet(both(has_down, near(1)), before, x, z + 1)
    greet(both(has_up, near(1)), before, x - 1, z + 1)
    one = lambda condition: jnp.where(condition, 1, 0)
    targets = 1 + 2 * one(has_down) + 2 * one(near(1)) + one(near(-1)) + 2 * one(both(has_down, near(-1)))
    pl.semaphore_wait(barrier, targets)

    width = kv.shape[2] // PIECES

    def copies(way, slot, piece, device, first=False):
        part = pl.ds(piece * width, width)
        src = kv_in.at[0, :, part] if first else kv.at[slot, :, part]
        yield pltpu.make_async_remote_copy(
            src_ref=src, dst_ref=kv.at[slot, :, part], send_sem=kv_send.at[way, slot, piece],
            recv_sem=kv_recv.at[slot, piece], device_id=device, device_id_type=MESH,
        )
        if piece == 0:
            yield pltpu.make_async_remote_copy(
                src_ref=seg_in if first else seg.at[slot], dst_ref=seg.at[slot], send_sem=seg_send.at[way, slot],
                recv_sem=seg_recv.at[slot], device_id=device, device_id_type=MESH,
            )

    def wait_piece(slot, piece):
        for copy in copies(OWN, slot, piece, (after, x, z)):
            copy.wait_recv()

    query_copy = pltpu.make_async_remote_copy(
        src_ref=q_in.at[0], dst_ref=q, send_sem=q_send, recv_sem=q_recv,
        device_id=(after, x, z), device_id_type=MESH,
    )

    def own_hops(act):
        for piece in range(PIECES):
            for copy in copies(OWN, me, piece, (after, x, z), True):
                act(copy)

    def first_hops(act):
        for piece in range(PIECES):
            hops = [(near(1), RIGHT, (after, x, z + 1)), (has_down, DOWN, (after, x + 1, z))]
            if piece == LAST:
                hops.append((both(has_down, near(-1)), LEFT, (after, x, z - 1)))
            else:
                hops.append((both(has_down, near(-1)), DIAGONAL, (after, x + 1, z - 1)))
            for condition, way, device in hops:
                @pl.when(condition)
                def _():
                    for copy in copies(way, me, piece, device, True):
                        act(copy)

    to = {RIGHT: (s, x, z + 1), DOWN: (s, x + 1, z), LEFT: (s, x, z - 1)}
    rounds = [[] for _ in range(columns)]
    for d, arrivals in enumerate(rounds):
        for piece in range(PIECES):
            last = piece == LAST
            inner = both(has_down, z > d) if last and d > 0 else has_down
            if d > 0:
                arrivals.append((z >= d, me - d, piece, [(near(1), RIGHT), (inner, DOWN)]))
                if last:
                    arrivals.append((both(has_down, near(d)), me + d, piece, [(near(-1), LEFT), (has_down, DOWN)]))
            for e in range(1, blocks):
                slot = me - e * columns
                sends = [(inner, DOWN)]
                if d == 0 and not last and e > 1:
                    sends.append((near(-1), LEFT))
                if last:
                    sends.append((both(near(1), z == d), RIGHT))
                arrivals.append((both(x >= e, z >= d), slot - d, piece, sends))
                if d > 0:
                    sends = [(has_down, DOWN)] if last else [(near(-1), LEFT)]
                    arrivals.append((both(x >= e, near(d)), slot + d, piece, sends))

    def pending(e, c, piece):
        if e == 0:
            down = both(has_down, c > 0) if piece == LAST else has_down
            return both(c <= z, jnp.logical_not(both(c < z, either(near(1), down))))
        if piece == LAST:
            level = either(both(has_down, either(c > 0, z == 0)), both(c == 0, near(1)))
            passed = jnp.where(c <= z, one(level), one(has_down))
        else:
            level = either(has_down, both(c == z, near(-1))) if e > 1 else has_down
            passed = jnp.where(c <= z, one(level), one(near(-1)))
        return both(x >= e, passed == 0)

    def passes(sends):
        needed = z < 0
        for condition, _ in sends:
            needed = either(needed, condition)
        return needed

    same_chip = lax.rem(s, 2) == 0

    def last_hops():
        own_hops(lambda copy: copy.start())
        query_copy.start()

    first_hops(lambda copy: copy.start())
    pl.when(same_chip)(last_hops)

    for slot in range(1, count):
        row, column = slot // columns, slot % columns
        later = both(x == row, z < column)

        @pl.when(either(x < row, later))
        def _():
            kv[slot, :, : LAST * width] = jnp.zeros((rows, LAST * width), kv.dtype)
            seg[slot] = jnp.zeros(seg.shape[1:], seg.dtype)

        @pl.when(either(x < row, both(later, jnp.logical_not(has_down))))
        def _():
            kv[slot, :, LAST * width :] = jnp.zeros((rows, width), kv.dtype)

    @pl.when(jnp.logical_not(same_chip))
    def _():
        first_hops(lambda copy: copy.wait_send())
        last_hops()

    query_heads = q.shape[1] // HEAD_SIZE
    key_heads = kv.shape[2] // (2 * HEAD_SIZE)
    group = query_heads // key_heads
    factor = math.log2(math.e) / math.sqrt(HEAD_SIZE)
    order = []
    for e in range(0, blocks, 2):
        for d in range(columns):
            pair = []
            for f in range(e, min(e + 2, blocks)):
                back, ahead = lax.rem(z - d + columns, columns), lax.rem(z + d, columns)
                c = back if f == 0 else jnp.where(2 * z < columns, ahead, back)
                pair.append((f, c, lax.rem(x - f + blocks, blocks) * columns + c))
            needed = either(x >= e + 1, both(x >= e, z >= d if e == 0 else x >= e))
            order.append((needed, pair))

    line = lax.broadcasted_iota(jnp.int32, (rows, rows), 0)
    lane = lax.broadcasted_iota(jnp.int32, (rows, rows), 1)

    def attend(n):
        needed, pair = order[n]

        @pl.when(needed)
        def _():
            for piece in range(PIECES):
                for e, c, slot in pair:
                    @pl.when(pending(e, c, piece))
                    def _():
                        wait_piece(slot, piece)
                if piece == 0:
                    own = jnp.broadcast_to(seg[me], (rows, rows))
                    labels = jnp.sum(jnp.where(line == lane, own, 0), axis=1, keepdims=True)
                    biases = []
                    for _, _, slot in pair:
                        allowed = both(slot * rows + lane <= me * rows + line, seg[slot] == labels)
                        biases.append(jnp.where(allowed, 0.0, MASKED))
                    bias = jnp.concatenate(biases, axis=1)
                    bias = jnp.concatenate([bias] * group, axis=0)
                for k in range(piece * key_heads // PIECES, (piece + 1) * key_heads // PIECES):
                    at = 2 * k * HEAD_SIZE
                    keys = jnp.concatenate([kv[slot, :, at : at + HEAD_SIZE] for _, _, slot in pair], axis=0)
                    values = jnp.concatenate(
                        [kv[slot, :, at + HEAD_SIZE : at + 2 * HEAD_SIZE] for _, _, slot in pair], axis=0
                    )
                    heads = range(group * k, group * (k + 1))
                    queries = jnp.concatenate([q[:, h * HEAD_SIZE : (h + 1) * HEAD_SIZE] for h in heads], axis=0)
                    scores = lax.dot_general(
                        queries, keys, (((1,), (1,)), ((), ())), preferred_element_type=jnp.float32
                    ) + bias
                    top = jnp.broadcast_to(jnp.max(scores, axis=1, keepdims=True), scores.shape)
                    if n > 0:
                        before_top = tops[k]
                        top = jnp.maximum(before_top, top)
                    weights = jnp.exp2((scores - top) * factor)
                    mixed = jnp.dot(weights.astype(jnp.bfloat16), values, preferred_element_type=jnp.float32)
                    if n > 0:
                        kept = jnp.exp2((before_top - top) * factor)
                        weights += totals[k] * kept
                        mixed += mixes[k] * kept
                    tops[k] = top
                    totals[k] = weights
                    mixes[k] = mixed

    for arrivals in rounds:
        for valid, slot, piece, sends in arrivals:
            @pl.when(both(valid, passes(sends)))
            def _():
                wait_piece(slot, piece)
                for condition, way in sends:
                    @pl.when(condition)
                    def _():
                        for copy in copies(way, slot, piece, to[way]):
                            copy.start()
    query_copy.wait_recv()
    for n in range(len(order)):
        attend(n)
    for k in range(key_heads):
        mixed = (mixes[k] / jnp.sum(totals[k], axis=1, keepdims=True)).astype(jnp.bfloat16)
        for g in range(group):
            h = group * k + g
            out_ref[0, :, h * HEAD_SIZE : (h + 1) * HEAD_SIZE] = mixed[g * rows : (g + 1) * rows]

    @pl.when(same_chip)
    def _():
        first_hops(lambda copy: copy.wait_send())

    own_hops(lambda copy: copy.wait_send())
    query_copy.wait_send()
    for valid, slot, piece, sends in sum(rounds, []):
        for condition, way in sends:
            @pl.when(both(valid, condition))
            def _():
                for copy in copies(way, slot, piece, to[way]):
                    copy.wait_send()


def per_device(queries, keys_values, segment_ids):
    sections, blocks, columns = (lax.axis_size(a) for a in ("section", "blk", "head"))
    rows = queries.shape[1]
    count = blocks * columns
    key_heads = keys_values.shape[2] // (2 * HEAD_SIZE)
    stacked = rows * queries.shape[2] // HEAD_SIZE // key_heads
    queries, keys_values, segment_ids = (
        pltpu.with_memory_space_constraint(a, pltpu.HBM) for a in (queries, keys_values, segment_ids)
    )
    return pl.pallas_call(
        functools.partial(kernel, sections, blocks, columns),
        out_shape=jax.ShapeDtypeStruct(queries.shape, jnp.bfloat16),
        in_specs=[pl.BlockSpec(memory_space=pltpu.HBM)] * 3,
        out_specs=pl.BlockSpec(memory_space=pltpu.VMEM),
        scratch_shapes=[
            pltpu.VMEM(queries.shape[1:], jnp.bfloat16),
            pltpu.VMEM((count,) + keys_values.shape[1:], jnp.bfloat16),
            pltpu.VMEM((count, 1, rows), jnp.int32),
            pltpu.VMEM((key_heads, stacked, min(blocks, 2) * rows), jnp.float32),
            pltpu.VMEM((key_heads, stacked, min(blocks, 2) * rows), jnp.float32),
            pltpu.VMEM((key_heads, stacked, HEAD_SIZE), jnp.float32),
            pltpu.SemaphoreType.DMA,
            pltpu.SemaphoreType.DMA,
            pltpu.SemaphoreType.DMA((5, count, PIECES)),
            pltpu.SemaphoreType.DMA((count, PIECES)),
            pltpu.SemaphoreType.DMA((5, count)),
            pltpu.SemaphoreType.DMA((count,)),
        ],
        compiler_params=pltpu.CompilerParams(
            collective_id=0, has_side_effects=True, vmem_limit_bytes=48 * 1024 * 1024
        ),
    )(queries, keys_values, segment_ids)


def solution(mesh):
    return jax.shard_map(
        per_device,
        mesh=mesh,
        in_specs=(
            P("section", ("blk", "head"), None),
            P("section", ("blk", "head"), None),
            P("section", ("blk", "head")),
        ),
        out_specs=P("section", ("blk", "head"), None),
        check_vma=False,
    )
```
